32 devices in a mesh: seq: 32 (over z, y, x, core).
Axes of the slice: x: 2, y: 2, z: 4, core: 2. Of those that a mesh axis runs over, the one named last changes fastest.
Arguments:
- tokens: bfloat16 [4096, 256], P('seq'), may hold values from -6 to 6
- cotangent: bfloat16 [4096, 256], P('seq'), may hold values from -6 to 6
- weight_in: bfloat16 [512, 1024], replicated, may hold values from -0.25 to 0.25
- bias_in: float32 [1024], replicated, may hold values from -4 to 4
- norm_gain: float32 [1024], replicated, may hold values from 0.1 to 1.9
- weight_out: bfloat16 [512, 1024], replicated, may hold values from -0.1875 to 0.1875
- bias_out: float32 [512], replicated, may hold values from -3 to 3
- gate_logit: float32 [512], replicated, may hold values from -1 to 3
Outputs:
- final_rows: bfloat16 [4096, 256], P('seq')
- grad_tokens: bfloat16 [4096, 256], P('seq')
- grad_weight_in: bfloat16 [512, 1024], replicated
- grad_weight_out: bfloat16 [512, 1024], replicated
- grad_bias_in: float32 [1024], replicated
- grad_norm_gain: float32 [1024], replicated
- grad_bias_out: float32 [512], replicated
- grad_gate_logit: float32 [512], replicated
The draws below stay inside these ranges and needn't reach their ends.
All inputs are finite; a program needn't handle non-finite values.
Results may differ from the reference program's by a relative error of at most 0.0075.
Values may be sent and summed in bfloat16 or wider, within the bound.
No kernel may reach another device: no remote copies, remote signals or barrier semaphores. Data moves between devices by JAX's collectives and lax.ppermute only.
A program may use at most 64 MiB of HBM per device.

```python
import jax
import jax.numpy as jnp
from jax import lax

D = 256
HID = 1024
LAYERS = 4
TOKENS = 4096
FIRST = 256


def block_levels(stream_key, shape, cuts, low, top_value):
    level = 1.0
    for position, parts in cuts:
        steps = jax.random.uniform(jax.random.fold_in(jax.random.fold_in(stream_key, 6), position), (parts,), jnp.float32, low / len(cuts), top_value / len(cuts))
        level = level * jnp.repeat(jnp.exp(steps), shape[position] // parts).reshape((-1,) + (1,) * (len(shape) - 1 - position))
    return level


def normal_values(rng, shape, scale, reach, split=(), kind=jnp.bfloat16):
    level = block_levels(rng, shape, split, -0.22, 0.18) if split else 1.0
    values = jax.random.normal(rng, shape, jnp.float32) * scale * level
    return jnp.minimum(jnp.maximum(values, -reach), reach).astype(kind)


def setup_inputs(seed: int = 0) -> dict:
    keys = jax.random.split(jax.random.key(seed), 9)
    return {
        "tokens": normal_values(keys[0], (TOKENS, D), 1.0, 6.0, ((0, 32),)),
        "cotangent": normal_values(keys[1], (TOKENS, D), 1.0, 6.0, ((0, 32),)),
        "weight_in": normal_values(keys[2], (2 * D, HID), (2 * D) ** -0.5, 0.25),
        "bias_in": normal_values(keys[3], (HID,), 1.0, 4.0, (), jnp.float32),
        "norm_gain": jnp.clip(1.0 + 0.18 * jax.random.normal(keys[4], (HID,), jnp.float32), 0.1, 1.9),
        "weight_out": normal_values(keys[5], (2 * D, HID), HID ** -0.5, 0.1875),
        "bias_out": normal_values(keys[6], (2 * D,), 0.5, 3.0, (), jnp.float32),
        "gate_logit": jnp.clip(jax.random.uniform(keys[7], (2 * D,), jnp.float32, -1.0, 3.0), -1.0, 3.0),
    }


epsilon = 1e-05
branch_scale = 0.25

def layer_forward(paired, params):
    weight_in, bias_in, norm_gain, weight_out, bias_out, gates_on = params
    pre_norm = jnp.dot(paired, weight_in, preferred_element_type=jnp.float32) + bias_in
    row_mean = lax.optimization_barrier(jnp.mean(pre_norm, axis=-1, keepdims=True))
    centred = pre_norm - row_mean
    variance = lax.optimization_barrier(jnp.mean(centred * centred, axis=-1, keepdims=True))
    inv_std = lax.rsqrt(variance + epsilon)
    normed = centred * inv_std
    scaled = normed * norm_gain
    hidden = jax.nn.gelu(scaled).astype(jnp.bfloat16)
    mixed = lax.dot_general(hidden, weight_out, (((1,), (1,)), ((), ())), preferred_element_type=jnp.float32) + bias_out
    result = (gates_on * paired.astype(jnp.float32) + branch_scale * mixed).astype(jnp.bfloat16)
    return (result, (normed, inv_std, scaled, hidden))

def layer_backward(paired, stored, grad_out, params):
    weight_in, bias_in, norm_gain, weight_out, bias_out, gates_on = params
    normed, inv_std, scaled, hidden = stored
    out_grads = grad_out.astype(jnp.float32)
    gate_terms = out_grads * paired.astype(jnp.float32)
    mix_grads = branch_scale * out_grads
    mix_cast = mix_grads.astype(jnp.bfloat16)
    hidden_grads = jnp.dot(mix_cast, weight_out, preferred_element_type=jnp.float32)
    slope = jax.vjp(jax.nn.gelu, scaled)[1]
    scaled_grads = slope(hidden_grads)[0]
    gain_terms = scaled_grads * normed
    normed_grads = scaled_grads * norm_gain
    pre_grads = inv_std * (normed_grads - lax.optimization_barrier(jnp.mean(normed_grads, axis=-1, keepdims=True)) - normed * lax.optimization_barrier(jnp.mean(normed_grads * normed, axis=-1, keepdims=True)))
    pre_cast = pre_grads.astype(jnp.bfloat16)
    back_in = lax.dot_general(pre_cast, weight_in, (((1,), (1,)), ((), ())), preferred_element_type=jnp.float32)
    pair_grads = (gates_on * out_grads + back_in).astype(jnp.bfloat16)
    return (pair_grads, (pre_grads, pre_cast, mix_grads, mix_cast, gain_terms, gate_terms))

def reference(tokens, cotangent, weight_in, bias_in, norm_gain, weight_out, bias_out, gate_logit):
    gates_on = jax.nn.sigmoid(gate_logit)
    params = (weight_in, bias_in, norm_gain, weight_out, bias_out, gates_on)
    pair_count = TOKENS // 2
    block_rows = min(pair_count, 4096)
    num_blocks = pair_count // block_rows

    def to_pairs(current, distance):
        viewed = current.reshape(TOKENS // (2 * distance), 2, distance, D)
        return jnp.concatenate([viewed[:, 0], viewed[:, 1]], axis=-1).reshape(pair_count, 2 * D)

    def from_pairs(joined, distance):
        viewed = joined.reshape(TOKENS // (2 * distance), distance, 2 * D)
        return jnp.stack([viewed[:, :, :D], viewed[:, :, D:]], axis=1).reshape(TOKENS, D)

    def forward_block(paired):
        return layer_forward(paired, params)[0]
    current = tokens
    kept_pairs = []
    for layer_num in range(LAYERS):
        distance = FIRST * 2 ** layer_num
        paired = to_pairs(current, distance)
        result = lax.map(forward_block, paired.reshape(num_blocks, block_rows, 2 * D))
        kept_pairs.append(paired)
        current = from_pairs(result.reshape(pair_count, 2 * D), distance)
    final_rows = current

    def block_step(carry, inputs):
        acc_in, acc_out, acc_bias, acc_gain, acc_bout, acc_gate = carry
        paired, grad_out = inputs
        stored = layer_forward(paired, params)[1]
        pair_grads, terms = layer_backward(paired, stored, grad_out, params)
        pre_grads, pre_cast, mix_grads, mix_cast, gain_terms, gate_terms = terms
        acc_in = acc_in + jnp.dot(paired.T, pre_cast, preferred_element_type=jnp.float32)
        acc_out = acc_out + jnp.dot(mix_cast.T, stored[3], preferred_element_type=jnp.float32)
        acc_bias = acc_bias + lax.optimization_barrier(jnp.sum(pre_grads, axis=0))
        acc_gain = acc_gain + lax.optimization_barrier(jnp.sum(gain_terms, axis=0))
        acc_bout = acc_bout + lax.optimization_barrier(jnp.sum(mix_grads, axis=0))
        acc_gate = acc_gate + lax.optimization_barrier(jnp.sum(gate_terms, axis=0))
        return ((acc_in, acc_out, acc_bias, acc_gain, acc_bout, acc_gate), pair_grads)
    carry = (jnp.zeros((2 * D, HID), jnp.float32), jnp.zeros((2 * D, HID), jnp.float32), jnp.zeros((HID,), jnp.float32), jnp.zeros((HID,), jnp.float32), jnp.zeros((2 * D,), jnp.float32), jnp.zeros((2 * D,), jnp.float32))
    grads_rows = cotangent
    for layer_num in reversed(range(LAYERS)):
        distance = FIRST * 2 ** layer_num
        grad_pairs = to_pairs(grads_rows, distance)
        inputs = (kept_pairs[layer_num].reshape(num_blocks, block_rows, 2 * D), grad_pairs.reshape(num_blocks, block_rows, 2 * D))
        carry, pair_grads = lax.scan(block_step, carry, inputs)
        grads_rows = from_pairs(pair_grads.reshape(pair_count, 2 * D), distance)
    scaling = float(pair_count) ** (-0.5)
    acc_in, acc_out, acc_bias, acc_gain, acc_bout, acc_gate = carry
    return (final_rows, grads_rows, (acc_in * scaling).astype(jnp.bfloat16), (acc_out * scaling).astype(jnp.bfloat16), acc_bias * scaling, acc_gain * scaling, acc_bout * scaling, acc_gate * gates_on * (1.0 - gates_on) * scaling)
```

```python
import functools

import jax
import jax.numpy as jnp
from jax import lax
from jax.experimental import pallas as pl
from jax.experimental.pallas import tpu as pltpu
from jax.sharding import PartitionSpec as P

LAYERS = 4
LANES = 128
CHUNK = 16

epsilon = 1e-05
branch_scale = 0.25
GELU_IN = 0.7978845608028654
GELU_CUBE = 0.044715

BF16 = jnp.bfloat16
F32 = jnp.float32


def split_small(total):
    high = total.astype(BF16).astype(F32)
    return jnp.concatenate([high, total - high], axis=0).astype(BF16)


def join_small(packed):
    wide = packed.astype(F32)
    rows = wide.shape[0] // 2
    return wide[:rows] + wide[rows:]


def layer_halves(blocks, layer):
    lower = [b for b in range(len(blocks)) if not b >> layer & 1]
    upper = [b for b in range(len(blocks)) if b >> layer & 1]
    left = jnp.concatenate([blocks[b] for b in lower], axis=0)
    right = jnp.concatenate([blocks[b] for b in upper], axis=0)
    return jnp.concatenate([left, right], axis=1), lower, upper


def layer_blocks(joined, lower, upper, height, width):
    blocks = [None] * (2 * len(lower))
    for i, b in enumerate(lower):
        blocks[b] = joined[i * height : (i + 1) * height, :width]
    for i, b in enumerate(upper):
        blocks[b] = joined[i * height : (i + 1) * height, width:]
    return blocks


def switch_kernel(
    place_ref, rows_ref, win_ref, bin_ref, gain_ref, wout_ref, bout_ref, gate_ref, msg_ref,
    pre_s, normed_s, slope_s, inv_s, hidden_s, cast_s, left_s, right_s, small_s,
):
    core = place_ref[0]
    total_rows, double = rows_ref.shape
    width = double // 2
    pairs = total_rows // 2
    count = 2**LAYERS
    height = total_rows // count
    hid = win_ref.shape[1]
    quarters = msg_ref.shape[0]
    gate = 1.0 / (1.0 + jnp.exp(-gate_ref[...]))
    bias_out = bout_ref[...]
    everything = rows_ref[...]
    blocks = [everything[b * height : (b + 1) * height, :width] for b in range(count)]
    grads = [everything[b * height : (b + 1) * height, width:] for b in range(count)]
    for layer in range(LAYERS):
        paired, lower, upper = layer_halves(blocks, layer)
        span = slice(layer * pairs, (layer + 1) * pairs)
        left_s[0, span, :] = paired
        pre_s[...] = jnp.dot(paired, win_ref[...], preferred_element_type=F32)
        for c in range(pairs // CHUNK):
            here = slice(c * CHUNK, (c + 1) * CHUNK)
            there = slice(layer * pairs + c * CHUNK, layer * pairs + (c + 1) * CHUNK)
            pre = pre_s[here, :] + bin_ref[...]
            centred = pre - jnp.mean(pre, axis=-1, keepdims=True)
            variance = jnp.mean(centred * centred, axis=-1, keepdims=True)
            inv_std = lax.rsqrt(variance + epsilon)
            normed = centred * inv_std
            scaled = normed * gain_ref[...]
            square = scaled * scaled
            bent = jnp.tanh(scaled * (GELU_IN + (GELU_IN * GELU_CUBE) * square))
            half = 0.5 + 0.5 * bent
            hidden_s[there, :] = (scaled * half).astype(BF16)
            slope_s[there, :] = half + (scaled * (0.5 - 0.5 * bent * bent)) * (
                GELU_IN + (3.0 * GELU_IN * GELU_CUBE) * square
            )
            normed_s[there, :] = normed
            inv_s[there, :] = jnp.broadcast_to(inv_std, (CHUNK, LANES))
        mixed = (
            lax.dot_general(
                hidden_s[span, :], wout_ref[...], (((1,), (1,)), ((), ())),
                preferred_element_type=F32,
            )
            + bias_out
        )
        result = (gate * paired.astype(F32) + branch_scale * mixed).astype(BF16)
        blocks = layer_blocks(result, lower, upper, height, width)

    sum_pre = jnp.zeros((1, hid), F32)
    sum_gain = jnp.zeros((1, hid), F32)
    sum_mix = jnp.zeros((1, 2 * width), F32)
    sum_gate = jnp.zeros((1, 2 * width), F32)
    for layer in reversed(range(LAYERS)):
        grad_out, lower, upper = layer_halves(grads, layer)
        span = slice(layer * pairs, (layer + 1) * pairs)
        out_grads = grad_out.astype(F32)
        paired = left_s[0, span, :].astype(F32)
        sum_gate += jnp.sum(out_grads * paired, axis=0, keepdims=True)
        mix_grads = branch_scale * out_grads
        sum_mix += jnp.sum(mix_grads, axis=0, keepdims=True)
        mix_cast = mix_grads.astype(BF16)
        left_s[1, span, :] = mix_cast
        pre_s[...] = jnp.dot(mix_cast, wout_ref[...], preferred_element_type=F32)
        part_pre = jnp.zeros((CHUNK, hid), F32)
        part_gain = jnp.zeros((CHUNK, hid), F32)
        for c in range(pairs // CHUNK):
            here = slice(c * CHUNK, (c + 1) * CHUNK)
            there = slice(layer * pairs + c * CHUNK, layer * pairs + (c + 1) * CHUNK)
            normed = normed_s[there, :]
            scaled_grads = slope_s[there, :] * pre_s[here, :]
            part_gain += scaled_grads * normed
            normed_grads = scaled_grads * gain_ref[...]
            mean_grad = jnp.mean(normed_grads, axis=-1, keepdims=True)
            mean_both = jnp.mean(normed_grads * normed, axis=-1, keepdims=True)
            pre_grads = inv_s[there, :1] * (normed_grads - mean_grad - normed * mean_both)
            part_pre += pre_grads
            cast_s[there, :] = pre_grads.astype(BF16)
        sum_pre += jnp.sum(part_pre, axis=0, keepdims=True)
        sum_gain += jnp.sum(part_gain, axis=0, keepdims=True)
        back_in = lax.dot_general(
            cast_s[span, :], win_ref[...], (((1,), (1,)), ((), ())), preferred_element_type=F32
        )
        result = (gate * out_grads + back_in).astype(BF16)
        grads = layer_blocks(result, lower, upper, height, width)

    @pl.when(core == 0)
    def _():
        right_s[...] = cast_s[...]

    @pl.when(core != 0)
    def _():
        right_s[...] = hidden_s[...]

    part_rows = 2 * width // quarters
    body = part_rows * hid // LANES
    for q in range(quarters):
        here = slice(q * part_rows, (q + 1) * part_rows)
        chosen = jnp.where(core == 0, left_s[0, :, here], left_s[1, :, here])
        part = lax.dot_general(
            chosen, right_s[...], (((0,), (0,)), ((), ())), preferred_element_type=F32
        ).astype(BF16)
        for k in range(hid // LANES):
            msg_ref[q, k * part_rows : (k + 1) * part_rows, :] = part[
                :, k * LANES : (k + 1) * LANES
            ]

    row = 0
    for total in (sum_pre, sum_gain, sum_mix, sum_gate):
        for k in range(total.shape[1] // LANES):
            small_s[row : row + 1, :] = total[:, k * LANES : (k + 1) * LANES]
            row += 1
    packed = split_small(small_s[...])
    own = height // 2
    for b in range(count):
        low, high = b % quarters, b // quarters
        for t, block in enumerate((blocks[b], grads[b])):
            wide = block.astype(F32)
            mine = jnp.where(core == 0, wide[:own], wide[own:])
            tall = jnp.concatenate(
                [mine[:, k * LANES : (k + 1) * LANES] for k in range(width // LANES)], axis=0
            )
            start = body + (high * 2 + t) * tall.shape[0]
            msg_ref[low, start : start + tall.shape[0], :] = tall.astype(BF16)
    for q in range(quarters):
        msg_ref[q, msg_ref.shape[1] - packed.shape[0] :, :] = packed


def plane_kernel(sizes, place_ref, got_ref, *out_refs):
    hid, part_rows, row_tile, small_rows = sizes
    mine = place_ref[2]
    sources = got_ref.shape[0]
    peers = len(out_refs)
    slabs = hid // LANES
    share = part_rows // peers
    body = slabs * part_rows
    small = join_small(got_ref[0, -2 * small_rows :, :])
    for s in range(1, sources):
        small = small + join_small(got_ref[s, -2 * small_rows :, :])
    packed = split_small(small)
    for k, out_ref in enumerate(out_refs):
        peer = mine ^ k
        for b in range(slabs):
            rows = pl.ds(pl.multiple_of(b * part_rows + peer * share, share), share)
            total = got_ref[0, rows, :].astype(F32)
            for s in range(1, sources):
                total = total + got_ref[s, rows, :].astype(F32)
            out_ref[b * share : (b + 1) * share, :] = total.astype(BF16)
        for s in range(sources):
            rows = pl.ds(pl.multiple_of(body + peer * row_tile, row_tile), row_tile)
            start = slabs * share + s * row_tile
            out_ref[start : start + row_tile, :] = got_ref[s, rows, :]
        out_ref[-2 * small_rows :, :] = packed


def column_kernel(sizes, scaling, place_ref, gate_ref, *refs):
    hid, part_rows, row_tile, small_rows, width, sources = sizes
    peers = (len(refs) - 7)
    got = refs[:peers]
    slice_ref, final_ref, grad_ref, pre_ref, gain_ref, mix_ref, gout_ref = refs[peers:]
    mine = place_ref[2]
    slabs = hid // LANES
    share = part_rows // peers

    def add(pick):
        terms = [pick(ref) for ref in got]
        while len(terms) > 1:
            terms = [terms[i] + terms[i + 1] for i in range(0, len(terms), 2)]
        return terms[0]

    for b in range(slabs):
        total = add(lambda ref: ref[b * share : (b + 1) * share, :].astype(F32))
        slice_ref[:, b * LANES : (b + 1) * LANES] = (total * scaling).astype(slice_ref.dtype)
    half = row_tile // 2
    own = half // (width // LANES)
    for k, ref in enumerate(got):
        peer = mine ^ k
        rows = pl.ds(pl.multiple_of(peer * (own * sources), own * sources), own * sources)
        for t, out_ref in enumerate((final_ref, grad_ref)):
            pieces = []
            for s in range(sources):
                start = slabs * share + s * row_tile + t * half
                tall = ref[start : start + half, :].astype(F32)
                pieces.append(
                    jnp.concatenate(
                        [tall[i * own : (i + 1) * own] for i in range(width // LANES)], axis=1
                    )
                )
            out_ref[rows, :] = jnp.concatenate(pieces, axis=0).astype(BF16)
    small = add(lambda ref: join_small(ref[-2 * small_rows :, :])) * scaling
    gate = 1.0 / (1.0 + jnp.exp(-gate_ref[...]))
    first = 0
    for out_ref in (pre_ref, gain_ref, mix_ref, gout_ref):
        count = out_ref.shape[0]
        part = small[first : first + count]
        if out_ref is gout_ref:
            part = part * gate * (1.0 - gate)
        out_ref[...] = part
        first += count


def gather_kernel(place_ref, *refs):
    *got, out_ref = refs
    mine = place_ref[2]
    share = got[0].shape[0]
    for k, ref in enumerate(got):
        rows = pl.ds(pl.multiple_of((mine ^ k) * share, share), share)
        for q in range(out_ref.shape[0]):
            out_ref[q, rows, :] = ref[...]


def order_kernel(place_ref, mine_ref, other_ref, first_ref, second_ref, sems):
    def move(first_src, second_src):
        one = pltpu.make_async_copy(first_src, first_ref, sems.at[0])
        two = pltpu.make_async_copy(second_src, second_ref, sems.at[1])
        one.start()
        two.start()
        one.wait()
        two.wait()

    @pl.when(place_ref[0] == 0)
    def _():
        move(mine_ref, other_ref)

    @pl.when(place_ref[0] != 0)
    def _():
        move(other_ref, mine_ref)


def bit_groups(devices, bits):
    masks = [sum(1 << b for i, b in enumerate(bits) if j >> i & 1) for j in range(2 ** len(bits))]
    every = sum(1 << b for b in bits)
    return [[base | m for m in masks] for base in range(devices) if not base & every]


def exchange(value, devices, bits):
    groups = None if 2 ** len(bits) == devices else bit_groups(devices, bits)
    return lax.all_to_all(value, "seq", 0, 0, axis_index_groups=groups)


def send(value, devices, mask):
    return lax.ppermute(value, "seq", [(i, i ^ mask) for i in range(devices)])


VMEM = pl.BlockSpec(memory_space=pltpu.VMEM)
SMEM = pl.BlockSpec(memory_space=pltpu.SMEM)
PARAMS = pltpu.CompilerParams(vmem_limit_bytes=48 * 1024 * 1024)


def per_device(tokens, cotangent, weight_in, bias_in, norm_gain, weight_out, bias_out, gate_logit):
    rows_dev, width = tokens.shape
    hid = weight_in.shape[1]
    devices = lax.axis_size("seq")
    top_bit = devices.bit_length() - 1
    index = lax.axis_index("seq").astype(jnp.int32)
    count = 2**LAYERS
    block_rows = rows_dev // count
    quarters = 4
    peers = 4
    place = jnp.stack([index & 1, index >> 1 & 3, index >> 3 & 3])
    both = jnp.concatenate(
        [tokens.reshape(count, block_rows, width), cotangent.reshape(count, block_rows, width)],
        axis=-1,
    )
    outgoing = jnp.broadcast_to(both[:, None], (count, 2, block_rows, 2 * width))
    outgoing = outgoing.reshape(2 * count, block_rows, 2 * width)
    top_bits = list(range(top_bit - LAYERS, top_bit))
    rows = exchange(outgoing, devices, [0] + top_bits).reshape(
        2 * count * block_rows, 2 * width
    )

    part_rows = 2 * width // quarters
    small_rows = (2 * hid + 4 * width) // LANES
    row_tile = 2 * block_rows * width // LANES
    pairs = count * block_rows
    msg_rows = part_rows * hid // LANES + (count // quarters) * row_tile + 2 * small_rows
    message = pl.pallas_call(
        switch_kernel,
        out_shape=jax.ShapeDtypeStruct((quarters, msg_rows, LANES), BF16),
        in_specs=[SMEM] + [VMEM] * 7,
        out_specs=VMEM,
        scratch_shapes=[
            pltpu.VMEM((pairs, hid), F32),
            pltpu.VMEM((LAYERS * pairs, hid), F32),
            pltpu.VMEM((LAYERS * pairs, hid), F32),
            pltpu.VMEM((LAYERS * pairs, LANES), F32),
            pltpu.VMEM((LAYERS * pairs, hid), BF16),
            pltpu.VMEM((LAYERS * pairs, hid), BF16),
            pltpu.VMEM((2, LAYERS * pairs, 2 * width), BF16),
            pltpu.VMEM((LAYERS * pairs, hid), BF16),
            pltpu.VMEM((small_rows, LANES), F32),
        ],
        compiler_params=PARAMS,
        name="switch_layers",
    )(
        place, rows, weight_in, bias_in[None], norm_gain[None], weight_out, bias_out[None],
        gate_logit[None],
    )

    got = exchange(message, devices, [1, 2])
    share = part_rows // peers
    out_rows = share * hid // LANES + quarters * row_tile + 2 * small_rows
    piece = jax.ShapeDtypeStruct((out_rows, LANES), BF16)
    pieces = pl.pallas_call(
        functools.partial(plane_kernel, (hid, part_rows, row_tile, small_rows)),
        out_shape=[piece] * peers,
        in_specs=[SMEM, VMEM],
        out_specs=[VMEM] * peers,
        compiler_params=PARAMS,
        name="plane_sum",
    )(place, got)
    arrived = [pieces[0]] + [send(pieces[k], devices, k << 3) for k in range(1, peers)]

    scaling = float(rows_dev * devices // 2) ** (-0.5)
    merged = top_bit == LAYERS + 1
    rows_shape = jax.ShapeDtypeStruct((rows_dev, width), BF16)
    slice_type = BF16 if merged else F32
    outs = pl.pallas_call(
        functools.partial(
            column_kernel,
            (hid, part_rows, row_tile, small_rows, width, quarters),
            scaling,
        ),
        out_shape=[
            jax.ShapeDtypeStruct((share, hid), slice_type),
            rows_shape,
            rows_shape,
            jax.ShapeDtypeStruct((hid // LANES, LANES), F32),
            jax.ShapeDtypeStruct((hid // LANES, LANES), F32),
            jax.ShapeDtypeStruct((2 * width // LANES, LANES), F32),
            jax.ShapeDtypeStruct((2 * width // LANES, LANES), F32),
        ],
        in_specs=[SMEM] + [VMEM] * (peers + 1),
        out_specs=[VMEM] * 7,
        compiler_params=PARAMS,
        name="column_sum",
    )(place, gate_logit.reshape(-1, LANES), *arrived)
    owned, final_rows, grad_rows, *small = outs
    if not merged:
        rest = bit_groups(devices, list(range(LAYERS + 1, top_bit)))
        owned, *small = lax.psum((owned, *small), "seq", axis_index_groups=rest)
        owned = owned.astype(BF16)
        final_rows, grad_rows = outward_rows(
            message, devices, top_bits, rows_dev, width, part_rows * hid // LANES
        )

    slices = [owned] + [send(owned, devices, k << 3) for k in range(1, peers)]
    spread = pl.pallas_call(
        gather_kernel,
        out_shape=jax.ShapeDtypeStruct((quarters, part_rows, hid), BF16),
        in_specs=[SMEM] + [VMEM] * peers,
        out_specs=VMEM,
        compiler_params=PARAMS,
        name="column_gather",
    )(place, *slices)
    whole = exchange(spread, devices, [1, 2]).reshape(2 * width, hid)
    other = send(whole, devices, 1)
    grad_weight = jax.ShapeDtypeStruct((2 * width, hid), BF16)
    grad_weight_in, grad_weight_out = pl.pallas_call(
        order_kernel,
        out_shape=[grad_weight] * 2,
        in_specs=[SMEM, VMEM, VMEM],
        out_specs=[pl.BlockSpec(memory_space=pl.ANY)] * 2,
        scratch_shapes=[pltpu.SemaphoreType.DMA((2,))],
        compiler_params=PARAMS,
        name="weight_order",
    )(place, whole, other)
    return (final_rows, grad_rows, grad_weight_in, grad_weight_out, *(s.reshape(-1) for s in small))


def outward_rows(message, devices, top_bits, rows_dev, width, body):
    quarters = message.shape[0]
    count = 2**LAYERS
    block_rows = rows_dev // count
    tail = count // quarters * 2 * block_rows * width // LANES
    shaped = message[:, body : body + tail].reshape(
        quarters, count // quarters, 2, width // LANES, block_rows, LANES
    )
    blocks = shaped.transpose(1, 0, 2, 4, 3, 5).reshape(count, 2, block_rows, width)
    back = exchange(blocks, devices, top_bits)
    return back[:, 0].reshape(rows_dev, width), back[:, 1].reshape(rows_dev, width)


def solution(mesh):
    placed = (P("seq", None), P("seq", None), P(), P(), P(), P(), P(), P())
    return jax.shard_map(
        per_device,
        mesh=mesh,
        in_specs=placed,
        out_specs=(P("seq", None), P("seq", None), P(), P(), P(), P(), P(), P()),
        check_vma=False,
    )
```

```python
import functools

import jax
import jax.numpy as jnp
from jax import lax
from jax.experimental import pallas as pl
from jax.experimental.pallas import tpu as pltpu
from jax.sharding import PartitionSpec as P

LAYERS = 4
LANES = 128
CHUNK = 16

epsilon = 1e-05
branch_scale = 0.25
GELU_IN = 0.7978845608028654
GELU_CUBE = 0.044715

BF16 = jnp.bfloat16
F32 = jnp.float32


def split_small(total):
    high = total.astype(BF16).astype(F32)
    return jnp.concatenate([high, total - high], axis=0).astype(BF16)


def join_small(packed):
    wide = packed.astype(F32)
    rows = wide.shape[0] // 2
    return wide[:rows] + wide[rows:]


def layer_halves(blocks, layer):
    lower = [b for b in range(len(blocks)) if not b >> layer & 1]
    upper = [b for b in range(len(blocks)) if b >> layer & 1]
    left = jnp.concatenate([blocks[b] for b in lower], axis=0)
    right = jnp.concatenate([blocks[b] for b in upper], axis=0)
    return jnp.concatenate([left, right], axis=1), lower, upper


def layer_blocks(joined, lower, upper, height, width):
    blocks = [None] * (2 * len(lower))
    for i, b in enumerate(lower):
        blocks[b] = joined[i * height : (i + 1) * height, :width]
    for i, b in enumerate(upper):
        blocks[b] = joined[i * height : (i + 1) * height, width:]
    return blocks


def entry_kernel(tokens_ref, cotangent_ref, out_ref):
    copies, keys, twins, height, double = out_ref.shape
    for key in range(keys):
        here = slice(key * height, (key + 1) * height)
        both = jnp.concatenate([tokens_ref[here, :], cotangent_ref[here, :]], axis=1)
        for copy in range(copies):
            for twin in range(twins):
                out_ref[copy, key, twin] = both


def keep_kernel(*refs):
    half = len(refs) // 2
    for source, target in zip(refs[:half], refs[half:]):
        target[...] = source[...]


def switch_kernel(
    place_ref, rows_ref, win_ref, bin_ref, gain_ref, wout_ref, bout_ref, gate_ref, msg_ref,
    pre_s, normed_s, slope_s, inv_s, hidden_s, cast_s, paired_s, mix_s, small_s, ends_s,
    left_s, right_s,
):
    core = place_ref[0]
    copy = place_ref[1]
    total_rows, double = rows_ref.shape
    width = double // 2
    pairs = total_rows // 2
    count = 2**LAYERS
    height = total_rows // count
    hid = win_ref.shape[1]
    keys = msg_ref.shape[0]
    gate = 1.0 / (1.0 + jnp.exp(-gate_ref[...]))
    bias_out = bout_ref[...]
    blocks = [rows_ref[b * height : (b + 1) * height, :width] for b in range(count)]
    for layer in range(LAYERS):
        paired, lower, upper = layer_halves(blocks, layer)
        span = slice(layer * pairs, (layer + 1) * pairs)
        paired_s[span, :] = paired
        pre_s[...] = jnp.dot(paired, win_ref[...], preferred_element_type=F32)
        for c in range(pairs // CHUNK):
            here = slice(c * CHUNK, (c + 1) * CHUNK)
            there = slice(layer * pairs + c * CHUNK, layer * pairs + (c + 1) * CHUNK)
            pre = pre_s[here, :] + bin_ref[...]
            centred = pre - jnp.mean(pre, axis=-1, keepdims=True)
            variance = jnp.mean(centred * centred, axis=-1, keepdims=True)
            inv_std = lax.rsqrt(variance + epsilon)
            normed = centred * inv_std
            scaled = normed * gain_ref[...]
            square = scaled * scaled
            bent = jnp.tanh(scaled * (GELU_IN + (GELU_IN * GELU_CUBE) * square))
            half = 0.5 + 0.5 * bent
            hidden_s[there, :] = (scaled * half).astype(BF16)
            slope_s[there, :] = half + (scaled * (0.5 - 0.5 * bent * bent)) * (
                GELU_IN + (3.0 * GELU_IN * GELU_CUBE) * square
            )
            normed_s[there, :] = normed
            inv_s[there, :] = jnp.broadcast_to(inv_std, (CHUNK, LANES))
        mixed = (
            lax.dot_general(
                hidden_s[span, :], wout_ref[...], (((1,), (1,)), ((), ())),
                preferred_element_type=F32,
            )
            + bias_out
        )
        result = (gate * paired.astype(F32) + branch_scale * mixed).astype(BF16)
        blocks = layer_blocks(result, lower, upper, height, width)
    for b in range(count):
        ends_s[0, b * height : (b + 1) * height, :] = blocks[b]

    blocks = [rows_ref[b * height : (b + 1) * height, width:] for b in range(count)]
    sum_pre = jnp.zeros((1, hid), F32)
    sum_gain = jnp.zeros((1, hid), F32)
    sum_mix = jnp.zeros((1, 2 * width), F32)
    sum_gate = jnp.zeros((1, 2 * width), F32)
    for layer in reversed(range(LAYERS)):
        grad_out, lower, upper = layer_halves(blocks, layer)
        span = slice(layer * pairs, (layer + 1) * pairs)
        out_grads = grad_out.astype(F32)
        paired = paired_s[span, :].astype(F32)
        sum_gate += jnp.sum(out_grads * paired, axis=0, keepdims=True)
        mix_grads = branch_scale * out_grads
        sum_mix += jnp.sum(mix_grads, axis=0, keepdims=True)
        mix_cast = mix_grads.astype(BF16)
        mix_s[span, :] = mix_cast
        pre_s[...] = jnp.dot(mix_cast, wout_ref[...], preferred_element_type=F32)
        part_pre = jnp.zeros((CHUNK, hid), F32)
        part_gain = jnp.zeros((CHUNK, hid), F32)
        for c in range(pairs // CHUNK):
            here = slice(c * CHUNK, (c + 1) * CHUNK)
            there = slice(layer * pairs + c * CHUNK, layer * pairs + (c + 1) * CHUNK)
            normed = normed_s[there, :]
            scaled_grads = slope_s[there, :] * pre_s[here, :]
            part_gain += scaled_grads * normed
            normed_grads = scaled_grads * gain_ref[...]
            mean_grad = jnp.mean(normed_grads, axis=-1, keepdims=True)
            mean_both = jnp.mean(normed_grads * normed, axis=-1, keepdims=True)
            pre_grads = inv_s[there, :1] * (normed_grads - mean_grad - normed * mean_both)
            part_pre += pre_grads
            cast_s[there, :] = pre_grads.astype(BF16)
        sum_pre += jnp.sum(part_pre, axis=0, keepdims=True)
        sum_gain += jnp.sum(part_gain, axis=0, keepdims=True)
        back_in = lax.dot_general(
            cast_s[span, :], win_ref[...], (((1,), (1,)), ((), ())), preferred_element_type=F32
        )
        result = (gate * out_grads + back_in).astype(BF16)
        blocks = layer_blocks(result, lower, upper, height, width)
    for b in range(count):
        ends_s[1, b * height : (b + 1) * height, :] = blocks[b]

    share = width // keys

    side = pl.ds(pl.multiple_of(copy * width, width), width)

    @pl.when(core == 0)
    def _():
        left_s[...] = paired_s[:, side]
        right_s[...] = cast_s[...]

    @pl.when(core != 0)
    def _():
        left_s[...] = mix_s[:, side]
        right_s[...] = hidden_s[...]

    for piece in range(width // LANES):
        part = lax.dot_general(
            left_s[:, piece * LANES : (piece + 1) * LANES], right_s[...],
            (((0,), (0,)), ((), ())), preferred_element_type=F32,
        ).astype(BF16)
        for i in range(LANES // share):
            key = piece * (LANES // share) + i
            for k in range(hid // LANES):
                msg_ref[key, k * share : (k + 1) * share, :] = part[
                    i * share : (i + 1) * share, k * LANES : (k + 1) * LANES
                ]

    row = 0
    for total in (sum_pre, sum_gain, sum_mix, sum_gate):
        for k in range(total.shape[1] // LANES):
            small_s[row : row + 1, :] = total[:, k * LANES : (k + 1) * LANES]
            row += 1
    packed = split_small(small_s[...])
    own = height // 2
    for key in range(keys):
        start = share * hid // LANES
        rows = pl.ds(pl.multiple_of((copy * keys + key) * height + core * own, own), own)
        for t in range(2):
            for k in range(width // LANES):
                msg_ref[key, start : start + own, :] = ends_s[
                    t, rows, k * LANES : (k + 1) * LANES
                ]
                start += own
        msg_ref[key, start:, :] = packed


def sum_kernel(
    sizes, scaling, got_ref, gate_ref,
    slice_ref, final_ref, grad_ref, pre_ref, gain_ref, mix_ref, gout_ref,
):
    share, own, width = sizes
    keys = got_ref.shape[0]
    hid = slice_ref.shape[1]
    for k in range(hid // LANES):
        here = slice(k * share, (k + 1) * share)
        total = got_ref[0, here, :].astype(F32)
        for key in range(1, keys):
            total += got_ref[key, here, :].astype(F32)
        slice_ref[:, k * LANES : (k + 1) * LANES] = (total * scaling).astype(slice_ref.dtype)
    start = share * hid // LANES
    for out_ref in (final_ref, grad_ref):
        for k in range(width // LANES):
            for key in range(keys):
                out_ref[key * own : (key + 1) * own, k * LANES : (k + 1) * LANES] = got_ref[
                    key, start : start + own, :
                ]
            start += own
    small = join_small(got_ref[0, start:, :])
    for key in range(1, keys):
        small = small + join_small(got_ref[key, start:, :])
    small = small * scaling
    gate = 1.0 / (1.0 + jnp.exp(-gate_ref[...]))
    first = 0
    for out_ref in (pre_ref, gain_ref, mix_ref, gout_ref):
        count = out_ref.shape[0]
        part = small[first : first + count]
        if out_ref is gout_ref:
            part = part * gate * (1.0 - gate)
        out_ref[...] = part
        first += count


def gather_kernel(place_ref, mine_ref, other_ref, out_ref):
    copy = place_ref[1]
    for key in range(out_ref.shape[0]):
        out_ref[key, copy] = mine_ref[...]
        out_ref[key, 1 - copy] = other_ref[...]


def order_kernel(place_ref, mine_ref, other_ref, first_ref, second_ref, sems):
    copies = mine_ref.shape[1]

    def move(first_src, second_src):
        moves = [
            pltpu.make_async_copy(source.at[:, copy], target.at[copy], sems.at[i, copy])
            for i, (source, target) in enumerate(
                ((first_src, first_ref), (second_src, second_ref))
            )
            for copy in range(copies)
        ]
        for one in moves:
            one.start()
        for one in moves:
            one.wait()

    @pl.when(place_ref[0] == 0)
    def _():
        move(mine_ref, other_ref)

    @pl.when(place_ref[0] != 0)
    def _():
        move(other_ref, mine_ref)


def bit_groups(devices, bits):
    masks = [sum(1 << b for i, b in enumerate(bits) if j >> i & 1) for j in range(2 ** len(bits))]
    every = sum(1 << b for b in bits)
    return [[base | m for m in masks] for base in range(devices) if not base & every]


def exchange(value, devices, bits):
    groups = None if 2 ** len(bits) == devices else bit_groups(devices, bits)
    return lax.all_to_all(value, "seq", 0, 0, axis_index_groups=groups)


def send(value, devices, mask):
    return lax.ppermute(value, "seq", [(i, i ^ mask) for i in range(devices)])


VMEM = pl.BlockSpec(memory_space=pltpu.VMEM)
SMEM = pl.BlockSpec(memory_space=pltpu.SMEM)
HBM = pl.BlockSpec(memory_space=pltpu.HBM)
PARAMS = pltpu.CompilerParams(vmem_limit_bytes=48 * 1024 * 1024)


def per_device(tokens, cotangent, weight_in, bias_in, norm_gain, weight_out, bias_out, gate_logit):
    rows_dev, width = tokens.shape
    hid = weight_in.shape[1]
    devices = lax.axis_size("seq")
    top_bit = devices.bit_length() - 1
    index = lax.axis_index("seq").astype(jnp.int32)
    top_bits = list(range(top_bit - LAYERS, top_bit))
    key_bits, copy_bit = top_bits[:-1], top_bits[-1]
    keys = 2 ** len(key_bits)
    own = rows_dev // keys
    place = jnp.stack([index & 1, index >> copy_bit & 1])

    kept = (weight_in, bias_in[None], norm_gain[None], weight_out, bias_out[None], gate_logit[None])
    kept = pl.pallas_call(
        keep_kernel,
        out_shape=[jax.ShapeDtypeStruct(k.shape, k.dtype) for k in kept],
        in_specs=[VMEM] * len(kept),
        out_specs=[VMEM] * len(kept),
        compiler_params=PARAMS,
        name="keep_weights",
    )(*kept)
    outgoing = pl.pallas_call(
        entry_kernel,
        out_shape=jax.ShapeDtypeStruct((2, keys, 2, own, 2 * width), BF16),
        in_specs=[VMEM] * 2,
        out_specs=VMEM,
        compiler_params=PARAMS,
        name="entry",
    )(tokens, cotangent)
    rows = exchange(outgoing.reshape(4 * keys, own, 2 * width), devices, [0] + top_bits)
    rows = rows.reshape(4 * keys * own, 2 * width)

    pairs = rows.shape[0] // 2
    share = width // keys
    small_rows = (2 * hid + 4 * width) // LANES
    msg_rows = share * hid // LANES + 2 * own * width // LANES + 2 * small_rows
    message = pl.pallas_call(
        switch_kernel,
        out_shape=jax.ShapeDtypeStruct((keys, msg_rows, LANES), BF16),
        in_specs=[SMEM] + [VMEM] * 7,
        out_specs=VMEM,
        scratch_shapes=[
            pltpu.VMEM((pairs, hid), F32),
            pltpu.VMEM((LAYERS * pairs, hid), F32),
            pltpu.VMEM((LAYERS * pairs, hid), F32),
            pltpu.VMEM((LAYERS * pairs, LANES), F32),
            pltpu.VMEM((LAYERS * pairs, hid), BF16),
            pltpu.VMEM((LAYERS * pairs, hid), BF16),
            pltpu.VMEM((LAYERS * pairs, 2 * width), BF16),
            pltpu.VMEM((LAYERS * pairs, 2 * width), BF16),
            pltpu.VMEM((small_rows, LANES), F32),
            pltpu.VMEM((2, 2 * pairs, width), BF16),
            pltpu.VMEM((LAYERS * pairs, width), BF16),
            pltpu.VMEM((LAYERS * pairs, hid), BF16),
        ],
        compiler_params=PARAMS,
        name="switch_layers",
    )(place, rows, *kept)

    got = exchange(message, devices, key_bits)
    scaling = float(rows_dev * devices // 2) ** (-0.5)
    rest = list(range(1, top_bit - LAYERS))
    rows_shape = jax.ShapeDtypeStruct((rows_dev, width), BF16)
    tall, short = hid // LANES, 2 * width // LANES
    owned, final_rows, grad_rows, *small = pl.pallas_call(
        functools.partial(sum_kernel, (share, own, width), scaling),
        out_shape=[jax.ShapeDtypeStruct((share, hid), F32 if rest else BF16)]
        + [rows_shape] * 2
        + [jax.ShapeDtypeStruct((n, LANES), F32) for n in (tall, tall, short, short)],
        in_specs=[VMEM] * 2,
        out_specs=[VMEM] * 7,
        compiler_params=PARAMS,
        name="key_sum",
    )(got, kept[-1].reshape(-1, LANES))
    if rest:
        owned, *small = lax.psum(
            (owned, *small), "seq", axis_index_groups=bit_groups(devices, rest)
        )
        owned = owned.astype(BF16)

    spread = pl.pallas_call(
        gather_kernel,
        out_shape=jax.ShapeDtypeStruct((keys, 2, share, hid), BF16),
        in_specs=[SMEM, VMEM, VMEM],
        out_specs=VMEM,
        compiler_params=PARAMS,
        name="copy_gather",
    )(place, owned, send(owned, devices, 1 << copy_bit))
    whole = exchange(spread, devices, key_bits)
    other = send(whole, devices, 1)
    ordered = jax.ShapeDtypeStruct((2, keys, share, hid), BF16)
    grad_weight_in, grad_weight_out = pl.pallas_call(
        order_kernel,
        out_shape=[ordered] * 2,
        in_specs=[SMEM, VMEM, VMEM],
        out_specs=[HBM] * 2,
        scratch_shapes=[pltpu.SemaphoreType.DMA((2, 2))],
        compiler_params=PARAMS,
        name="weight_order",
    )(place, whole, other)
    return (
        final_rows,
        grad_rows,
        grad_weight_in.reshape(2 * width, hid),
        grad_weight_out.reshape(2 * width, hid),
        *(s.reshape(-1) for s in small),
    )


def solution(mesh):
    placed = (P("seq", None), P("seq", None), P(), P(), P(), P(), P(), P())
    return jax.shard_map(
        per_device,
        mesh=mesh,
        in_specs=placed,
        out_specs=(P("seq", None), P("seq", None), P(), P(), P(), P(), P(), P()),
        check_vma=False,
    )
```

```python
import functools

import jax
import jax.numpy as jnp
from jax import lax
from jax.experimental import pallas as pl
from jax.experimental.pallas import tpu as pltpu
from jax.sharding import PartitionSpec as P

LAYERS = 4
LANES = 128
CHUNK = 16
TILE = 256

epsilon = 1e-05
branch_scale = 0.25
GELU_IN = 0.7978845608028654
GELU_CUBE = 0.044715

BF16 = jnp.bfloat16
F32 = jnp.float32


def split_small(total):
    high = total.astype(BF16).astype(F32)
    return jnp.concatenate([high, total - high], axis=0).astype(BF16)


def join_small(packed):
    wide = packed.astype(F32)
    rows = wide.shape[0] // 2
    return wide[:rows] + wide[rows:]


def layer_halves(blocks, layer):
    lower = [b for b in range(len(blocks)) if not b >> layer & 1]
    upper = [b for b in range(len(blocks)) if b >> layer & 1]
    left = jnp.concatenate([blocks[b] for b in lower], axis=0)
    right = jnp.concatenate([blocks[b] for b in upper], axis=0)
    return jnp.concatenate([left, right], axis=1), lower, upper


def layer_blocks(joined, lower, upper, height, width):
    blocks = [None] * (2 * len(lower))
    for i, b in enumerate(lower):
        blocks[b] = joined[i * height : (i + 1) * height, :width]
    for i, b in enumerate(upper):
        blocks[b] = joined[i * height : (i + 1) * height, width:]
    return blocks


def keep_kernel(*refs):
    half = len(refs) // 2
    for source, target in zip(refs[:half], refs[half:]):
        target[...] = source[...]


def fold_lanes(tile):
    return sum(tile[:, k : k + LANES] for k in range(0, tile.shape[1], LANES))


def widen(stat):
    return jnp.concatenate([stat] * (TILE // LANES), axis=1)


def row_total(folded):
    return jnp.sum(folded, axis=-1, keepdims=True)


def switch_kernel(
    place_ref, rows_ref, win_ref, bin_ref, gain_ref, wout_ref, bout_ref, gate_ref, msg_ref,
    pre_s, normed_s, slope_s, inv_s, stat_s, both_s, side_s, small_s, ends_s,
):
    core = place_ref[0]
    copy = place_ref[1]
    twins, count, own, double = rows_ref.shape
    width = double // 2
    height = twins * own
    pairs = count * height // 2
    hid = win_ref.shape[1]
    keys = msg_ref.shape[0]
    columns = [slice(c, c + TILE) for c in range(0, hid, TILE)]
    chunks = [slice(r, r + CHUNK) for r in range(0, pairs, CHUNK)]
    gate = 1.0 / (1.0 + jnp.exp(-gate_ref[...]))
    bias_out = bout_ref[...]

    def below(layer, here):
        return slice(layer * pairs + here.start, layer * pairs + here.stop)

    blocks = [
        jnp.concatenate([rows_ref[twin, b, :, :width] for twin in range(twins)], axis=0)
        for b in range(count)
    ]
    for layer in range(LAYERS):
        paired, lower, upper = layer_halves(blocks, layer)
        span = slice(layer * pairs, (layer + 1) * pairs)
        for side in range(2):
            side_s[0, side, span, :] = paired[:, side * width : (side + 1) * width]

        def project(column):
            pre_s[:, column] = jnp.dot(
                paired, win_ref[:, column], preferred_element_type=F32
            ) + bin_ref[:, column]

        def gather_stats(column):
            for here in chunks:
                pre = pre_s[here, column]
                if column.start == 0:
                    shift = row_total(fold_lanes(pre)) * (1.0 / TILE)
                    stat_s[0, here, :] = jnp.broadcast_to(shift, (CHUNK, LANES))
                    moved = pre - shift
                    stat_s[1, here, :] = fold_lanes(moved)
                    stat_s[2, here, :] = fold_lanes(moved * moved)
                else:
                    moved = pre - widen(stat_s[0, here, :])
                    stat_s[1, here, :] += fold_lanes(moved)
                    stat_s[2, here, :] += fold_lanes(moved * moved)

        project(columns[0])
        for now, column in zip(columns[1:], columns):
            project(now)
            gather_stats(column)
        gather_stats(columns[-1])
        for here in chunks:
            drift = row_total(stat_s[1, here, :]) * (1.0 / hid)
            square = row_total(stat_s[2, here, :]) * (1.0 / hid)
            inv_std = lax.rsqrt(square - drift * drift + epsilon)
            stat_s[0, here, :] = stat_s[0, here, :] + drift
            inv_s[below(layer, here), :] = jnp.broadcast_to(inv_std, (CHUNK, LANES))
        def activate(column):
            for here in chunks:
                there = below(layer, here)
                normed = (pre_s[here, column] - widen(stat_s[0, here, :])) * widen(
                    inv_s[there, :]
                )
                scaled = normed * gain_ref[:, column]
                square = scaled * scaled
                bent = jnp.tanh(scaled * (GELU_IN + (GELU_IN * GELU_CUBE) * square))
                half = 0.5 + 0.5 * bent
                both_s[1, there, column] = (scaled * half).astype(BF16)
                slope_s[there, column] = half + (scaled * (0.5 - 0.5 * bent * bent)) * (
                    GELU_IN + (3.0 * GELU_IN * GELU_CUBE) * square
                )
                normed_s[there, column] = normed

        activate(columns[0])
        mixed = None
        for i, column in enumerate(columns):
            if i + 1 < len(columns):
                activate(columns[i + 1])
            part = lax.dot_general(
                both_s[1, span, column], wout_ref[:, column], (((1,), (1,)), ((), ())),
                preferred_element_type=F32,
            )
            mixed = part if mixed is None else mixed + part
        result = (
            gate * paired.astype(F32) + branch_scale * (mixed + bias_out)
        ).astype(BF16)
        blocks = layer_blocks(result, lower, upper, height, width)
    for b in range(count):
        ends_s[0, b * height : (b + 1) * height, :] = blocks[b]

    blocks = [
        jnp.concatenate([rows_ref[twin, b, :, width:] for twin in range(twins)], axis=0)
        for b in range(count)
    ]
    sum_pre = [jnp.zeros((1, TILE), F32) for _ in columns]
    sum_gain = [jnp.zeros((1, TILE), F32) for _ in columns]
    sum_mix = jnp.zeros((1, 2 * width), F32)
    sum_gate = jnp.zeros((1, 2 * width), F32)
    for layer in reversed(range(LAYERS)):
        grad_out, lower, upper = layer_halves(blocks, layer)
        span = slice(layer * pairs, (layer + 1) * pairs)
        out_grads = grad_out.astype(F32)
        paired = jnp.concatenate([side_s[0, side, span, :] for side in range(2)], axis=1)
        sum_gate += jnp.sum(out_grads * paired.astype(F32), axis=0, keepdims=True)
        mix_grads = branch_scale * out_grads
        sum_mix += jnp.sum(mix_grads, axis=0, keepdims=True)
        mix_cast = mix_grads.astype(BF16)
        for side in range(2):
            side_s[1, side, span, :] = mix_cast[:, side * width : (side + 1) * width]

        def project(column):
            pre_s[:, column] = jnp.dot(
                mix_cast, wout_ref[:, column], preferred_element_type=F32
            )

        def gather_stats(i, column):
            gains = jnp.zeros((CHUNK, TILE), F32)
            for here in chunks:
                there = below(layer, here)
                normed = normed_s[there, column]
                scaled_grads = slope_s[there, column] * pre_s[here, column]
                gains += scaled_grads * normed
                normed_grads = scaled_grads * gain_ref[:, column]
                pre_s[here, column] = normed_grads
                first = fold_lanes(normed_grads)
                second = fold_lanes(normed_grads * normed)
                if i == 0:
                    stat_s[1, here, :] = first
                    stat_s[2, here, :] = second
                else:
                    stat_s[1, here, :] += first
                    stat_s[2, here, :] += second
            sum_gain[i] += jnp.sum(gains, axis=0, keepdims=True)

        project(columns[0])
        for i, now in enumerate(columns[1:]):
            project(now)
            gather_stats(i, columns[i])
        gather_stats(len(columns) - 1, columns[-1])
        for here in chunks:
            for k in (1, 2):
                mean = row_total(stat_s[k, here, :]) * (1.0 / hid)
                stat_s[k, here, :] = jnp.broadcast_to(mean, (CHUNK, LANES))
        def finish(i, column):
            total = jnp.zeros((CHUNK, TILE), F32)
            for here in chunks:
                there = below(layer, here)
                pre_grads = widen(inv_s[there, :]) * (
                    pre_s[here, column]
                    - widen(stat_s[1, here, :])
                    - normed_s[there, column] * widen(stat_s[2, here, :])
                )
                total += pre_grads
                both_s[0, there, column] = pre_grads.astype(BF16)
            sum_pre[i] += jnp.sum(total, axis=0, keepdims=True)

        finish(0, columns[0])
        back_in = None
        for i, column in enumerate(columns):
            if i + 1 < len(columns):
                finish(i + 1, columns[i + 1])
            part = lax.dot_general(
                both_s[0, span, column], win_ref[:, column], (((1,), (1,)), ((), ())),
                preferred_element_type=F32,
            )
            back_in = part if back_in is None else back_in + part
        result = (gate * out_grads + back_in).astype(BF16)
        blocks = layer_blocks(result, lower, upper, height, width)
    for b in range(count):
        ends_s[1, b * height : (b + 1) * height, :] = blocks[b]

    share = width // keys
    for piece in range(width // LANES):
        part = lax.dot_general(
            side_s[core, copy, :, piece * LANES : (piece + 1) * LANES], both_s[core],
            (((0,), (0,)), ((), ())), preferred_element_type=F32,
        ).astype(BF16)
        for i in range(LANES // share):
            key = piece * (LANES // share) + i
            for k in range(hid // LANES):
                msg_ref[key, k * share : (k + 1) * share, :] = part[
                    i * share : (i + 1) * share, k * LANES : (k + 1) * LANES
                ]

    row = 0
    for total in (*sum_pre, *sum_gain, sum_mix, sum_gate):
        for k in range(total.shape[1] // LANES):
            small_s[row : row + 1, :] = total[:, k * LANES : (k + 1) * LANES]
            row += 1
    packed = split_small(small_s[...])
    for key in range(keys):
        start = share * hid // LANES
        rows = pl.ds(pl.multiple_of((copy * keys + key) * height + core * own, own), own)
        for t in range(2):
            for k in range(width // LANES):
                msg_ref[key, start : start + own, :] = ends_s[
                    t, rows, k * LANES : (k + 1) * LANES
                ]
                start += own
        msg_ref[key, start:, :] = packed


def sum_kernel(
    sizes, scaling, got_ref, gate_ref,
    slice_ref, final_ref, grad_ref, pre_ref, gain_ref, mix_ref, gout_ref,
):
    share, own, width = sizes
    keys = got_ref.shape[0]
    hid = slice_ref.shape[1]
    for k in range(hid // LANES):
        here = slice(k * share, (k + 1) * share)
        total = got_ref[0, here, :].astype(F32)
        for key in range(1, keys):
            total += got_ref[key, here, :].astype(F32)
        slice_ref[:, k * LANES : (k + 1) * LANES] = (total * scaling).astype(slice_ref.dtype)
    start = share * hid // LANES
    for out_ref in (final_ref, grad_ref):
        for k in range(width // LANES):
            for key in range(keys):
                out_ref[key * own : (key + 1) * own, k * LANES : (k + 1) * LANES] = got_ref[
                    key, start : start + own, :
                ]
            start += own
    small = join_small(got_ref[0, start:, :])
    for key in range(1, keys):
        small = small + join_small(got_ref[key, start:, :])
    small = small * scaling
    gate = 1.0 / (1.0 + jnp.exp(-gate_ref[...]))
    first = 0
    for out_ref in (pre_ref, gain_ref, mix_ref, gout_ref):
        count = out_ref.shape[0]
        part = small[first : first + count]
        if out_ref is gout_ref:
            part = part * gate * (1.0 - gate)
        out_ref[...] = part
        first += count


def gather_kernel(place_ref, mine_ref, other_ref, out_ref):
    copy = place_ref[1]
    for key in range(out_ref.shape[0]):
        out_ref[key, copy] = mine_ref[...]
        out_ref[key, 1 - copy] = other_ref[...]


def move_weight(source_ref, target_ref, sems):
    keys, copies = source_ref.shape[:2]
    moves = [
        pltpu.make_async_copy(
            source_ref.at[key, copy], target_ref.at[copy, key], sems.at[copies * key + copy]
        )
        for key in range(keys)
        for copy in range(copies)
    ]
    for move in moves:
        move.start()
    for move in moves:
        move.wait()


def mine_kernel(place_ref, mine_ref, first_ref, second_ref, sems):
    for core, out_ref in enumerate((first_ref, second_ref)):

        @pl.when(place_ref[0] == core)
        def _():
            move_weight(mine_ref, out_ref, sems)


def other_kernel(place_ref, other_ref, first_in, second_in, first_ref, second_ref, sems):
    for core, out_ref in enumerate((second_ref, first_ref)):

        @pl.when(place_ref[0] == core)
        def _():
            move_weight(other_ref, out_ref, sems)


def bit_groups(devices, bits):
    masks = [sum(1 << b for i, b in enumerate(bits) if j >> i & 1) for j in range(2 ** len(bits))]
    every = sum(1 << b for b in bits)
    return [[base | m for m in masks] for base in range(devices) if not base & every]


def exchange(value, devices, bits):
    groups = None if 2 ** len(bits) == devices else bit_groups(devices, bits)
    return lax.all_to_all(value, "seq", 0, 0, axis_index_groups=groups)


def send(value, devices, mask):
    return lax.ppermute(value, "seq", [(i, i ^ mask) for i in range(devices)])


VMEM = pl.BlockSpec(memory_space=pltpu.VMEM)
SMEM = pl.BlockSpec(memory_space=pltpu.SMEM)
HBM = pl.BlockSpec(memory_space=pltpu.HBM)
PARAMS = pltpu.CompilerParams(vmem_limit_bytes=4 * 1024 * 1024)
WIDE = pltpu.CompilerParams(vmem_limit_bytes=32 * 1024 * 1024)


def compute(place, rows, kept):
    hid = kept[0].shape[1]
    twins, count, own, double = rows.shape
    width = double // 2
    keys = count // 2
    pairs = twins * count * own // 2
    share = width // keys
    small_rows = (2 * hid + 4 * width) // LANES
    msg_rows = share * hid // LANES + 2 * own * width // LANES + 2 * small_rows
    return pl.pallas_call(
        switch_kernel,
        out_shape=jax.ShapeDtypeStruct((keys, msg_rows, LANES), BF16),
        in_specs=[SMEM] + [VMEM] * 7,
        out_specs=VMEM,
        scratch_shapes=[
            pltpu.VMEM((pairs, hid), F32),
            pltpu.VMEM((LAYERS * pairs, hid), F32),
            pltpu.VMEM((LAYERS * pairs, hid), F32),
            pltpu.VMEM((LAYERS * pairs, LANES), F32),
            pltpu.VMEM((3, pairs, LANES), F32),
            pltpu.VMEM((2, LAYERS * pairs, hid), BF16),
            pltpu.VMEM((2, 2, LAYERS * pairs, width), BF16),
            pltpu.VMEM((small_rows, LANES), F32),
            pltpu.VMEM((2, 2 * pairs, width), BF16),
        ],
        compiler_params=WIDE,
        name="switch_layers",
    )(place, rows, *kept)


def per_device(tokens, cotangent, weight_in, bias_in, norm_gain, weight_out, bias_out, gate_logit):
    rows_dev, width = tokens.shape
    hid = weight_in.shape[1]
    devices = lax.axis_size("seq")
    top_bit = devices.bit_length() - 1
    index = lax.axis_index("seq").astype(jnp.int32)
    top_bits = list(range(top_bit - LAYERS, top_bit))
    key_bits, copy_bit = top_bits[:-1], top_bits[-1]
    keys = 2 ** len(key_bits)
    own = rows_dev // keys
    place = jnp.stack([index & 1, index >> copy_bit & 1])

    kept = (weight_in, bias_in[None], norm_gain[None], weight_out, bias_out[None], gate_logit[None])
    kept = pl.pallas_call(
        keep_kernel,
        out_shape=[jax.ShapeDtypeStruct(k.shape, k.dtype) for k in kept],
        in_specs=[VMEM] * len(kept),
        out_specs=[VMEM] * len(kept),
        compiler_params=PARAMS,
        name="keep_weights",
    )(*kept)
    both = jnp.concatenate([tokens, cotangent], axis=-1).reshape(keys, own, 2 * width)
    rows = exchange(jnp.concatenate([both, both], axis=0), devices, top_bits)
    rows = lax.all_gather(rows, "seq", axis=0, axis_index_groups=bit_groups(devices, [0]))

    message = compute(place, rows, kept)
    share = width // keys
    got = exchange(message, devices, key_bits)
    scaling = float(rows_dev * devices // 2) ** (-0.5)
    rest = list(range(1, top_bit - LAYERS))
    rows_shape = jax.ShapeDtypeStruct((rows_dev, width), BF16)
    tall, short = hid // LANES, 2 * width // LANES
    owned, final_rows, grad_rows, *small = pl.pallas_call(
        functools.partial(sum_kernel, (share, own, width), scaling),
        out_shape=[jax.ShapeDtypeStruct((share, hid), F32 if rest else BF16)]
        + [rows_shape] * 2
        + [jax.ShapeDtypeStruct((n, LANES), F32) for n in (tall, tall, short, short)],
        in_specs=[VMEM] * 2,
        out_specs=[VMEM] * 7,
        compiler_params=PARAMS,
        name="key_sum",
    )(got, kept[5].reshape(-1, LANES))
    if rest:
        owned, *small = lax.psum(
            (owned, *small), "seq", axis_index_groups=bit_groups(devices, rest)
        )
        owned = owned.astype(BF16)

    spread = pl.pallas_call(
        gather_kernel,
        out_shape=jax.ShapeDtypeStruct((keys, 2, share, hid), BF16),
        in_specs=[SMEM, VMEM, VMEM],
        out_specs=VMEM,
        compiler_params=PARAMS,
        name="copy_gather",
    )(place, owned, send(owned, devices, 1 << copy_bit))
    whole = exchange(spread, devices, key_bits)
    other = send(whole, devices, 1)
    ordered = jax.ShapeDtypeStruct((2, keys, share, hid), BF16)
    weights = pl.pallas_call(
        mine_kernel,
        out_shape=[ordered] * 2,
        in_specs=[SMEM, VMEM],
        out_specs=[HBM] * 2,
        scratch_shapes=[pltpu.SemaphoreType.DMA((2 * keys,))],
        compiler_params=PARAMS,
        name="mine_out",
    )(place, whole)
    grad_weight_in, grad_weight_out = pl.pallas_call(
        other_kernel,
        out_shape=[ordered] * 2,
        in_specs=[SMEM, VMEM, HBM, HBM],
        out_specs=[HBM] * 2,
        scratch_shapes=[pltpu.SemaphoreType.DMA((2 * keys,))],
        input_output_aliases={2: 0, 3: 1},
        compiler_params=PARAMS,
        name="other_out",
    )(place, other, *weights)
    return (
        final_rows,
        grad_rows,
        grad_weight_in.reshape(2 * width, hid),
        grad_weight_out.reshape(2 * width, hid),
        *(s.reshape(-1) for s in small),
    )


def solution(mesh):
    placed = (P("seq", None), P("seq", None), P(), P(), P(), P(), P(), P())
    return jax.shard_map(
        per_device,
        mesh=mesh,
        in_specs=placed,
        out_specs=(P("seq", None), P("seq", None), P(), P(), P(), P(), P(), P()),
        check_vma=False,
    )
```

```python
import functools

import jax
import jax.numpy as jnp
from jax import lax
from jax.experimental import pallas as pl
from jax.experimental.pallas import tpu as pltpu
from jax.sharding import PartitionSpec as P

LAYERS = 4
LANES = 128
CHUNK = 16
TILE = 256

epsilon = 1e-05
branch_scale = 0.25
GELU_IN = 0.7978845608028654
GELU_CUBE = 0.044715

BF16 = jnp.bfloat16
F32 = jnp.float32


def split_small(total):
    high = total.astype(BF16).astype(F32)
    return jnp.concatenate([high, total - high], axis=0).astype(BF16)


def join_small(packed):
    wide = packed.astype(F32)
    rows = wide.shape[0] // 2
    return wide[:rows] + wide[rows:]


def layer_halves(blocks, layer):
    lower = [b for b in range(len(blocks)) if not b >> layer & 1]
    upper = [b for b in range(len(blocks)) if b >> layer & 1]
    left = jnp.concatenate([blocks[b] for b in lower], axis=0)
    right = jnp.concatenate([blocks[b] for b in upper], axis=0)
    return jnp.concatenate([left, right], axis=1), lower, upper


def layer_blocks(joined, lower, upper, height, width):
    blocks = [None] * (2 * len(lower))
    for i, b in enumerate(lower):
        blocks[b] = joined[i * height : (i + 1) * height, :width]
    for i, b in enumerate(upper):
        blocks[b] = joined[i * height : (i + 1) * height, width:]
    return blocks


def keep_kernel(*refs):
    half = len(refs) // 2
    for source, target in zip(refs[:half], refs[half:]):
        target[...] = source[...]


def fold_lanes(tile):
    return sum(tile[:, k : k + LANES] for k in range(0, tile.shape[1], LANES))


def widen(stat):
    return jnp.concatenate([stat] * (TILE // LANES), axis=1)


def row_total(folded):
    return jnp.sum(folded, axis=-1, keepdims=True)


def switch_kernel(
    place_ref, rows_ref, win_ref, bin_ref, gain_ref, wout_ref, bout_ref, gate_ref,
    mine_ref, send_ref, tail_ref, small_ref,
    pre_s, normed_s, slope_s, inv_s, stat_s, both_s, side_s, ends_s,
):
    core = place_ref[0]
    copy = place_ref[1]
    count, height, double = rows_ref.shape
    width = double // 2
    pairs = count * height // 2
    hid = win_ref.shape[1]
    keys = tail_ref.shape[0]
    columns = [slice(c, c + TILE) for c in range(0, hid, TILE)]
    chunks = [slice(r, r + CHUNK) for r in range(0, pairs, CHUNK)]
    gate = 1.0 / (1.0 + jnp.exp(-gate_ref[...]))
    bias_out = bout_ref[...]

    def below(layer, here):
        return slice(layer * pairs + here.start, layer * pairs + here.stop)

    blocks = [rows_ref[b, :, :width] for b in range(count)]
    for layer in range(LAYERS):
        paired, lower, upper = layer_halves(blocks, layer)
        span = slice(layer * pairs, (layer + 1) * pairs)
        for side in range(2):
            side_s[0, side, span, :] = paired[:, side * width : (side + 1) * width]

        def project(column):
            pre_s[:, column] = jnp.dot(
                paired, win_ref[:, column], preferred_element_type=F32
            ) + bin_ref[:, column]

        def gather_stats(column):
            for here in chunks:
                pre = pre_s[here, column]
                if column.start == 0:
                    shift = row_total(fold_lanes(pre)) * (1.0 / TILE)
                    stat_s[0, here, :] = jnp.broadcast_to(shift, (CHUNK, LANES))
                    moved = pre - shift
                    stat_s[1, here, :] = fold_lanes(moved)
                    stat_s[2, here, :] = fold_lanes(moved * moved)
                else:
                    moved = pre - widen(stat_s[0, here, :])
                    stat_s[1, here, :] += fold_lanes(moved)
                    stat_s[2, here, :] += fold_lanes(moved * moved)

        project(columns[0])
        for now, column in zip(columns[1:], columns):
            project(now)
            gather_stats(column)
        gather_stats(columns[-1])
        for here in chunks:
            drift = row_total(stat_s[1, here, :]) * (1.0 / hid)
            square = row_total(stat_s[2, here, :]) * (1.0 / hid)
            inv_std = lax.rsqrt(square - drift * drift + epsilon)
            stat_s[0, here, :] = stat_s[0, here, :] + drift
            inv_s[below(layer, here), :] = jnp.broadcast_to(inv_std, (CHUNK, LANES))
        def activate(column):
            for here in chunks:
                there = below(layer, here)
                normed = (pre_s[here, column] - widen(stat_s[0, here, :])) * widen(
                    inv_s[there, :]
                )
                scaled = normed * gain_ref[:, column]
                square = scaled * scaled
                bent = jnp.tanh(scaled * (GELU_IN + (GELU_IN * GELU_CUBE) * square))
                half = 0.5 + 0.5 * bent
                both_s[1, there, column] = (scaled * half).astype(BF16)
                slope_s[there, column] = half + (scaled * (0.5 - 0.5 * bent * bent)) * (
                    GELU_IN + (3.0 * GELU_IN * GELU_CUBE) * square
                )
                normed_s[there, column] = normed

        activate(columns[0])
        mixed = None
        for i, column in enumerate(columns):
            if i + 1 < len(columns):
                activate(columns[i + 1])
            part = lax.dot_general(
                both_s[1, span, column], wout_ref[:, column], (((1,), (1,)), ((), ())),
                preferred_element_type=F32,
            )
            mixed = part if mixed is None else mixed + part
        result = (
            gate * paired.astype(F32) + branch_scale * (mixed + bias_out)
        ).astype(BF16)
        blocks = layer_blocks(result, lower, upper, height, width)
    for b in range(count):
        ends_s[0, b * height : (b + 1) * height, :] = blocks[b]

    blocks = [rows_ref[b, :, width:] for b in range(count)]
    sum_pre = [jnp.zeros((1, TILE), F32) for _ in columns]
    sum_gain = [jnp.zeros((1, TILE), F32) for _ in columns]
    sum_mix = jnp.zeros((1, 2 * width), F32)
    sum_gate = jnp.zeros((1, 2 * width), F32)
    for layer in reversed(range(LAYERS)):
        grad_out, lower, upper = layer_halves(blocks, layer)
        span = slice(layer * pairs, (layer + 1) * pairs)
        out_grads = grad_out.astype(F32)
        paired = jnp.concatenate([side_s[0, side, span, :] for side in range(2)], axis=1)
        sum_gate += jnp.sum(out_grads * paired.astype(F32), axis=0, keepdims=True)
        mix_grads = branch_scale * out_grads
        sum_mix += jnp.sum(mix_grads, axis=0, keepdims=True)
        mix_cast = mix_grads.astype(BF16)
        for side in range(2):
            side_s[1, side, span, :] = mix_cast[:, side * width : (side + 1) * width]

        def project(column):
            pre_s[:, column] = jnp.dot(
                mix_cast, wout_ref[:, column], preferred_element_type=F32
            )

        def gather_stats(i, column):
            gains = jnp.zeros((CHUNK, TILE), F32)
            for here in chunks:
                there = below(layer, here)
                normed = normed_s[there, column]
                scaled_grads = slope_s[there, column] * pre_s[here, column]
                gains += scaled_grads * normed
                normed_grads = scaled_grads * gain_ref[:, column]
                pre_s[here, column] = normed_grads
                first = fold_lanes(normed_grads)
                second = fold_lanes(normed_grads * normed)
                if i == 0:
                    stat_s[1, here, :] = first
                    stat_s[2, here, :] = second
                else:
                    stat_s[1, here, :] += first
                    stat_s[2, here, :] += second
            sum_gain[i] += jnp.sum(gains, axis=0, keepdims=True)

        project(columns[0])
        for i, now in enumerate(columns[1:]):
            project(now)
            gather_stats(i, columns[i])
        gather_stats(len(columns) - 1, columns[-1])
        for here in chunks:
            for k in (1, 2):
                mean = row_total(stat_s[k, here, :]) * (1.0 / hid)
                stat_s[k, here, :] = jnp.broadcast_to(mean, (CHUNK, LANES))
        def finish(i, column):
            total = jnp.zeros((CHUNK, TILE), F32)
            for here in chunks:
                there = below(layer, here)
                pre_grads = widen(inv_s[there, :]) * (
                    pre_s[here, column]
                    - widen(stat_s[1, here, :])
                    - normed_s[there, column] * widen(stat_s[2, here, :])
                )
                total += pre_grads
                both_s[0, there, column] = pre_grads.astype(BF16)
            sum_pre[i] += jnp.sum(total, axis=0, keepdims=True)

        finish(0, columns[0])
        back_in = None
        for i, column in enumerate(columns):
            if i + 1 < len(columns):
                finish(i + 1, columns[i + 1])
            part = lax.dot_general(
                both_s[0, span, column], win_ref[:, column], (((1,), (1,)), ((), ())),
                preferred_element_type=F32,
            )
            back_in = part if back_in is None else back_in + part
        result = (gate * out_grads + back_in).astype(BF16)
        blocks = layer_blocks(result, lower, upper, height, width)
    for b in range(count):
        ends_s[1, b * height : (b + 1) * height, :] = blocks[b]

    share = width // keys
    slab = share * hid // LANES
    for weight, out_ref in ((1 - core, send_ref), (core, mine_ref)):
        for piece in range(width // LANES):
            part = lax.dot_general(
                side_s[weight, copy, :, piece * LANES : (piece + 1) * LANES], both_s[weight],
                (((0,), (0,)), ((), ())), preferred_element_type=F32,
            ).astype(out_ref.dtype)
            for i in range(LANES // share):
                for k in range(hid // LANES):
                    start = (piece * (LANES // share) + i) * slab + k * share
                    out_ref[start : start + share, :] = part[
                        i * share : (i + 1) * share, k * LANES : (k + 1) * LANES
                    ]

    row = 0
    for total in (*sum_pre, *sum_gain, sum_mix, sum_gate):
        for k in range(total.shape[1] // LANES):
            small_ref[row : row + 1, :] = total[:, k * LANES : (k + 1) * LANES]
            row += 1
    send_ref[keys * slab :, :] = split_small(small_ref[...])
    for key in range(keys):
        start = 0
        rows = pl.ds(pl.multiple_of((copy * keys + key) * height, height), height)
        for t in range(2):
            for k in range(width // LANES):
                tail_ref[key, start : start + height, :] = ends_s[
                    t, rows, k * LANES : (k + 1) * LANES
                ]
                start += height


def core_kernel(mine_ref, tail_ref, small_ref, other_ref, msg_ref):
    keys, tail = tail_ref.shape[:2]
    slab = mine_ref.shape[0] // keys
    small = join_small(split_small(small_ref[...])) + join_small(other_ref[keys * slab :, :])
    packed = split_small(small)
    for key in range(keys):
        here = slice(key * slab, (key + 1) * slab)
        msg_ref[key, :slab, :] = (mine_ref[here, :] + other_ref[here, :].astype(F32)).astype(BF16)
        msg_ref[key, slab : slab + tail, :] = tail_ref[key]
        msg_ref[key, slab + tail :, :] = packed


def sum_kernel(
    sizes, scaling, got_ref, gate_ref,
    slice_ref, final_ref, grad_ref, pre_ref, gain_ref, mix_ref, gout_ref,
):
    share, own, width = sizes
    keys = got_ref.shape[0]
    hid = slice_ref.shape[1]
    for k in range(hid // LANES):
        here = slice(k * share, (k + 1) * share)
        total = got_ref[0, here, :].astype(F32)
        for key in range(1, keys):
            total += got_ref[key, here, :].astype(F32)
        slice_ref[:, k * LANES : (k + 1) * LANES] = (total * scaling).astype(slice_ref.dtype)
    start = share * hid // LANES
    for out_ref in (final_ref, grad_ref):
        for k in range(width // LANES):
            for key in range(keys):
                out_ref[key * own : (key + 1) * own, k * LANES : (k + 1) * LANES] = got_ref[
                    key, start : start + own, :
                ]
            start += own
    small = join_small(got_ref[0, start:, :])
    for key in range(1, keys):
        small = small + join_small(got_ref[key, start:, :])
    small = small * scaling
    gate = 1.0 / (1.0 + jnp.exp(-gate_ref[...]))
    first = 0
    for out_ref in (pre_ref, gain_ref, mix_ref, gout_ref):
        count = out_ref.shape[0]
        part = small[first : first + count]
        if out_ref is gout_ref:
            part = part * gate * (1.0 - gate)
        out_ref[...] = part
        first += count


def gather_kernel(place_ref, mine_ref, other_ref, out_ref):
    copy = place_ref[1]
    for key in range(out_ref.shape[0]):
        out_ref[key, copy] = mine_ref[...]
        out_ref[key, 1 - copy] = other_ref[...]


def move_weight(source_ref, target_ref, sems):
    keys, copies = source_ref.shape[:2]
    moves = [
        pltpu.make_async_copy(
            source_ref.at[key, copy], target_ref.at[copy, key], sems.at[copies * key + copy]
        )
        for key in range(keys)
        for copy in range(copies)
    ]
    for move in moves:
        move.start()
    for move in moves:
        move.wait()


def mine_kernel(place_ref, mine_ref, first_ref, second_ref, sems):
    for core, out_ref in enumerate((first_ref, second_ref)):

        @pl.when(place_ref[0] == core)
        def _():
            move_weight(mine_ref, out_ref, sems)


def other_kernel(place_ref, other_ref, first_in, second_in, first_ref, second_ref, sems):
    for core, out_ref in enumerate((second_ref, first_ref)):

        @pl.when(place_ref[0] == core)
        def _():
            move_weight(other_ref, out_ref, sems)


def bit_groups(devices, bits):
    masks = [sum(1 << b for i, b in enumerate(bits) if j >> i & 1) for j in range(2 ** len(bits))]
    every = sum(1 << b for b in bits)
    return [[base | m for m in masks] for base in range(devices) if not base & every]


def exchange(value, devices, bits):
    groups = None if 2 ** len(bits) == devices else bit_groups(devices, bits)
    return lax.all_to_all(value, "seq", 0, 0, axis_index_groups=groups)


def send(value, devices, mask):
    return lax.ppermute(value, "seq", [(i, i ^ mask) for i in range(devices)])


VMEM = pl.BlockSpec(memory_space=pltpu.VMEM)
SMEM = pl.BlockSpec(memory_space=pltpu.SMEM)
HBM = pl.BlockSpec(memory_space=pltpu.HBM)
PARAMS = pltpu.CompilerParams(vmem_limit_bytes=4 * 1024 * 1024)
WIDE = pltpu.CompilerParams(vmem_limit_bytes=32 * 1024 * 1024)


def compute(place, rows, kept):
    hid = kept[0].shape[1]
    count, own, double = rows.shape
    width = double // 2
    keys = count // 2
    pairs = count * own // 2
    slab = width // keys * hid // LANES
    tail = 2 * own * width // LANES
    small_rows = (2 * hid + 4 * width) // LANES
    return pl.pallas_call(
        switch_kernel,
        out_shape=[
            jax.ShapeDtypeStruct((keys * slab, LANES), F32),
            jax.ShapeDtypeStruct((keys * slab + 2 * small_rows, LANES), BF16),
            jax.ShapeDtypeStruct((keys, tail, LANES), BF16),
            jax.ShapeDtypeStruct((small_rows, LANES), F32),
        ],
        in_specs=[SMEM] + [VMEM] * 7,
        out_specs=[VMEM] * 4,
        scratch_shapes=[
            pltpu.VMEM((pairs, hid), F32),
            pltpu.VMEM((LAYERS * pairs, hid), F32),
            pltpu.VMEM((LAYERS * pairs, hid), F32),
            pltpu.VMEM((LAYERS * pairs, LANES), F32),
            pltpu.VMEM((3, pairs, LANES), F32),
            pltpu.VMEM((2, LAYERS * pairs, hid), BF16),
            pltpu.VMEM((2, 2, LAYERS * pairs, width), BF16),
            pltpu.VMEM((2, 2 * pairs, width), BF16),
        ],
        compiler_params=WIDE,
        name="switch_layers",
    )(place, rows, *kept)


def per_device(tokens, cotangent, weight_in, bias_in, norm_gain, weight_out, bias_out, gate_logit):
    rows_dev, width = tokens.shape
    hid = weight_in.shape[1]
    devices = lax.axis_size("seq")
    top_bit = devices.bit_length() - 1
    index = lax.axis_index("seq").astype(jnp.int32)
    top_bits = list(range(top_bit - LAYERS, top_bit))
    key_bits, copy_bit = top_bits[:-1], top_bits[-1]
    keys = 2 ** len(key_bits)
    own = rows_dev // keys
    place = jnp.stack([index & 1, index >> copy_bit & 1])

    kept = (weight_in, bias_in[None], norm_gain[None], weight_out, bias_out[None], gate_logit[None])
    kept = pl.pallas_call(
        keep_kernel,
        out_shape=[jax.ShapeDtypeStruct(k.shape, k.dtype) for k in kept],
        in_specs=[VMEM] * len(kept),
        out_specs=[VMEM] * len(kept),
        compiler_params=PARAMS,
        name="keep_weights",
    )(*kept)
    both = jnp.concatenate([tokens, cotangent], axis=-1).reshape(keys, own, 2 * width)
    rows = exchange(jnp.concatenate([both, both], axis=0), devices, top_bits)

    mine, sent, tail, small = compute(place, rows, kept)
    message = pl.pallas_call(
        core_kernel,
        out_shape=jax.ShapeDtypeStruct(
            (keys, mine.shape[0] // keys + tail.shape[1] + 2 * small.shape[0], LANES), BF16
        ),
        in_specs=[VMEM] * 4,
        out_specs=VMEM,
        compiler_params=PARAMS,
        name="core_sum",
    )(mine, tail, small, send(sent, devices, 1))
    share = width // keys
    got = exchange(message, devices, key_bits)
    scaling = float(rows_dev * devices // 2) ** (-0.5)
    rest = list(range(1, top_bit - LAYERS))
    rows_shape = jax.ShapeDtypeStruct((rows_dev, width), BF16)
    tall, short = hid // LANES, 2 * width // LANES
    owned, final_rows, grad_rows, *small = pl.pallas_call(
        functools.partial(sum_kernel, (share, own, width), scaling),
        out_shape=[jax.ShapeDtypeStruct((share, hid), F32 if rest else BF16)]
        + [rows_shape] * 2
        + [jax.ShapeDtypeStruct((n, LANES), F32) for n in (tall, tall, short, short)],
        in_specs=[VMEM] * 2,
        out_specs=[VMEM] * 7,
        compiler_params=PARAMS,
        name="key_sum",
    )(got, kept[5].reshape(-1, LANES))
    if rest:
        owned, *small = lax.psum(
            (owned, *small), "seq", axis_index_groups=bit_groups(devices, rest)
        )
        owned = owned.astype(BF16)

    spread = pl.pallas_call(
        gather_kernel,
        out_shape=jax.ShapeDtypeStruct((keys, 2, share, hid), BF16),
        in_specs=[SMEM, VMEM, VMEM],
        out_specs=VMEM,
        compiler_params=PARAMS,
        name="copy_gather",
    )(place, owned, send(owned, devices, 1 << copy_bit))
    whole = exchange(spread, devices, key_bits)
    other = send(whole, devices, 1)
    ordered = jax.ShapeDtypeStruct((2, keys, share, hid), BF16)
    weights = pl.pallas_call(
        mine_kernel,
        out_shape=[ordered] * 2,
        in_specs=[SMEM, VMEM],
        out_specs=[HBM] * 2,
        scratch_shapes=[pltpu.SemaphoreType.DMA((2 * keys,))],
        compiler_params=PARAMS,
        name="mine_out",
    )(place, whole)
    grad_weight_in, grad_weight_out = pl.pallas_call(
        other_kernel,
        out_shape=[ordered] * 2,
        in_specs=[SMEM, VMEM, HBM, HBM],
        out_specs=[HBM] * 2,
        scratch_shapes=[pltpu.SemaphoreType.DMA((2 * keys,))],
        input_output_aliases={2: 0, 3: 1},
        compiler_params=PARAMS,
        name="other_out",
    )(place, other, *weights)
    return (
        final_rows,
        grad_rows,
        grad_weight_in.reshape(2 * width, hid),
        grad_weight_out.reshape(2 * width, hid),
        *(s.reshape(-1) for s in small),
    )


def solution(mesh):
    placed = (P("seq", None), P("seq", None), P(), P(), P(), P(), P(), P())
    return jax.shard_map(
        per_device,
        mesh=mesh,
        in_specs=placed,
        out_specs=(P("seq", None), P("seq", None), P(), P(), P(), P(), P(), P()),
        check_vma=False,
    )
```

```python
import functools

import jax
import jax.numpy as jnp
from jax import lax
from jax.experimental import pallas as pl
from jax.experimental.pallas import tpu as pltpu
from jax.sharding import PartitionSpec as P

LAYERS = 4
LANES = 128
CHUNK = 16
TILE = 256

epsilon = 1e-05
branch_scale = 0.25
GELU_IN = 0.7978845608028654
GELU_CUBE = 0.044715

BF16 = jnp.bfloat16
F32 = jnp.float32


def split_small(total):
    high = total.astype(BF16).astype(F32)
    return jnp.concatenate([high, total - high], axis=0).astype(BF16)


def join_small(packed):
    wide = packed.astype(F32)
    rows = wide.shape[0] // 2
    return wide[:rows] + wide[rows:]


def layer_halves(blocks, layer):
    lower = [b for b in range(len(blocks)) if not b >> layer & 1]
    upper = [b for b in range(len(blocks)) if b >> layer & 1]
    left = jnp.concatenate([blocks[b] for b in lower], axis=0)
    right = jnp.concatenate([blocks[b] for b in upper], axis=0)
    return jnp.concatenate([left, right], axis=1), lower, upper


def layer_blocks(joined, lower, upper, height, width):
    blocks = [None] * (2 * len(lower))
    for i, b in enumerate(lower):
        blocks[b] = joined[i * height : (i + 1) * height, :width]
    for i, b in enumerate(upper):
        blocks[b] = joined[i * height : (i + 1) * height, width:]
    return blocks


def keep_kernel(*refs):
    half = len(refs) // 2
    for source, target in zip(refs[:half], refs[half:]):
        target[...] = source[...]


def fold_lanes(tile):
    return sum(tile[:, k : k + LANES] for k in range(0, tile.shape[1], LANES))


def widen(stat):
    return jnp.concatenate([stat] * (TILE // LANES), axis=1)


def row_total(folded):
    return jnp.sum(folded, axis=-1, keepdims=True)


def core_place():
    return lax.axis_index("seq") & 1


def copy_place():
    return lax.axis_index("seq") >> (lax.axis_size("seq").bit_length() - 2) & 1


def switch_kernel(
    rows_ref, win_ref, bin_ref, gain_ref, wout_ref, bout_ref, gate_ref,
    send_ref, both_s, side_s, ends_s, small_ref,
    pre_s, normed_s, slope_s, inv_s, stat_s,
):
    core, copy = core_place(), copy_place()
    count, height, double = rows_ref.shape
    width = double // 2
    pairs = count * height // 2
    hid = win_ref.shape[1]
    keys = count // 2
    columns = [slice(c, c + TILE) for c in range(0, hid, TILE)]
    chunks = [slice(r, r + CHUNK) for r in range(0, pairs, CHUNK)]
    gate = 1.0 / (1.0 + jnp.exp(-gate_ref[...]))
    bias_out = bout_ref[...]

    def below(layer, here):
        return slice(layer * pairs + here.start, layer * pairs + here.stop)

    blocks = [rows_ref[b, :, :width] for b in range(count)]
    for layer in range(LAYERS):
        paired, lower, upper = layer_halves(blocks, layer)
        span = slice(layer * pairs, (layer + 1) * pairs)
        for side in range(2):
            side_s[0, side, span, :] = paired[:, side * width : (side + 1) * width]

        def project(column):
            pre_s[:, column] = jnp.dot(
                paired, win_ref[:, column], preferred_element_type=F32
            ) + bin_ref[:, column]

        def gather_stats(column):
            for here in chunks:
                pre = pre_s[here, column]
                if column.start == 0:
                    shift = row_total(fold_lanes(pre)) * (1.0 / TILE)
                    stat_s[0, here, :] = jnp.broadcast_to(shift, (CHUNK, LANES))
                    moved = pre - shift
                    stat_s[1, here, :] = fold_lanes(moved)
                    stat_s[2, here, :] = fold_lanes(moved * moved)
                else:
                    moved = pre - widen(stat_s[0, here, :])
                    stat_s[1, here, :] += fold_lanes(moved)
                    stat_s[2, here, :] += fold_lanes(moved * moved)

        project(columns[0])
        for now, column in zip(columns[1:], columns):
            project(now)
            gather_stats(column)
        gather_stats(columns[-1])
        for here in chunks:
            drift = row_total(stat_s[1, here, :]) * (1.0 / hid)
            square = row_total(stat_s[2, here, :]) * (1.0 / hid)
            inv_std = lax.rsqrt(square - drift * drift + epsilon)
            stat_s[0, here, :] = stat_s[0, here, :] + drift
            inv_s[below(layer, here), :] = jnp.broadcast_to(inv_std, (CHUNK, LANES))
        def activate(column):
            for here in chunks:
                there = below(layer, here)
                normed = (pre_s[here, column] - widen(stat_s[0, here, :])) * widen(
                    inv_s[there, :]
                )
                scaled = normed * gain_ref[:, column]
                square = scaled * scaled
                bent = jnp.tanh(scaled * (GELU_IN + (GELU_IN * GELU_CUBE) * square))
                half = 0.5 + 0.5 * bent
                both_s[1, there, column] = (scaled * half).astype(BF16)
                slope_s[there, column] = half + (scaled * (0.5 - 0.5 * bent * bent)) * (
                    GELU_IN + (3.0 * GELU_IN * GELU_CUBE) * square
                )
                normed_s[there, column] = normed

        activate(columns[0])
        mixed = None
        for i, column in enumerate(columns):
            if i + 1 < len(columns):
                activate(columns[i + 1])
            part = lax.dot_general(
                both_s[1, span, column], wout_ref[:, column], (((1,), (1,)), ((), ())),
                preferred_element_type=F32,
            )
            mixed = part if mixed is None else mixed + part
        result = (
            gate * paired.astype(F32) + branch_scale * (mixed + bias_out)
        ).astype(BF16)
        blocks = layer_blocks(result, lower, upper, height, width)
    for b in range(count):
        ends_s[0, b * height : (b + 1) * height, :] = blocks[b]

    blocks = [rows_ref[b, :, width:] for b in range(count)]
    sum_pre = [jnp.zeros((1, TILE), F32) for _ in columns]
    sum_gain = [jnp.zeros((1, TILE), F32) for _ in columns]
    sum_mix = jnp.zeros((1, 2 * width), F32)
    sum_gate = jnp.zeros((1, 2 * width), F32)
    for layer in reversed(range(LAYERS)):
        grad_out, lower, upper = layer_halves(blocks, layer)
        span = slice(layer * pairs, (layer + 1) * pairs)
        out_grads = grad_out.astype(F32)
        paired = jnp.concatenate([side_s[0, side, span, :] for side in range(2)], axis=1)
        sum_gate += jnp.sum(out_grads * paired.astype(F32), axis=0, keepdims=True)
        mix_grads = branch_scale * out_grads
        sum_mix += jnp.sum(mix_grads, axis=0, keepdims=True)
        mix_cast = mix_grads.astype(BF16)
        for side in range(2):
            side_s[1, side, span, :] = mix_cast[:, side * width : (side + 1) * width]

        def project(column):
            pre_s[:, column] = jnp.dot(
                mix_cast, wout_ref[:, column], preferred_element_type=F32
            )

        def gather_stats(i, column):
            gains = jnp.zeros((CHUNK, TILE), F32)
            for here in chunks:
                there = below(layer, here)
                normed = normed_s[there, column]
                scaled_grads = slope_s[there, column] * pre_s[here, column]
                gains += scaled_grads * normed
                normed_grads = scaled_grads * gain_ref[:, column]
                pre_s[here, column] = normed_grads
                first = fold_lanes(normed_grads)
                second = fold_lanes(normed_grads * normed)
                if i == 0:
                    stat_s[1, here, :] = first
                    stat_s[2, here, :] = second
                else:
                    stat_s[1, here, :] += first
                    stat_s[2, here, :] += second
            sum_gain[i] += jnp.sum(gains, axis=0, keepdims=True)

        project(columns[0])
        for i, now in enumerate(columns[1:]):
            project(now)
            gather_stats(i, columns[i])
        gather_stats(len(columns) - 1, columns[-1])
        for here in chunks:
            for k in (1, 2):
                mean = row_total(stat_s[k, here, :]) * (1.0 / hid)
                stat_s[k, here, :] = jnp.broadcast_to(mean, (CHUNK, LANES))
        def finish(i, column):
            total = jnp.zeros((CHUNK, TILE), F32)
            for here in chunks:
                there = below(layer, here)
                pre_grads = widen(inv_s[there, :]) * (
                    pre_s[here, column]
                    - widen(stat_s[1, here, :])
                    - normed_s[there, column] * widen(stat_s[2, here, :])
                )
                total += pre_grads
                both_s[0, there, column] = pre_grads.astype(BF16)
            sum_pre[i] += jnp.sum(total, axis=0, keepdims=True)

        finish(0, columns[0])
        back_in = None
        for i, column in enumerate(columns):
            if i + 1 < len(columns):
                finish(i + 1, columns[i + 1])
            part = lax.dot_general(
                both_s[0, span, column], win_ref[:, column], (((1,), (1,)), ((), ())),
                preferred_element_type=F32,
            )
            back_in = part if back_in is None else back_in + part
        result = (gate * out_grads + back_in).astype(BF16)
        blocks = layer_blocks(result, lower, upper, height, width)
    for b in range(count):
        ends_s[1, b * height : (b + 1) * height, :] = blocks[b]

    weight_part(side_s.at[1 - core, copy], both_s.at[1 - core], send_ref)
    row = 0
    for total in (*sum_pre, *sum_gain, sum_mix, sum_gate):
        for k in range(total.shape[1] // LANES):
            small_ref[row : row + 1, :] = total[:, k * LANES : (k + 1) * LANES]
            row += 1
    packed = split_small(small_ref[...])
    send_ref[send_ref.shape[0] - packed.shape[0] :, :] = packed


def weight_part(left_ref, right_ref, out_ref):
    width, hid = left_ref.shape[1], right_ref.shape[1]
    share = 2 * width // 2**LAYERS
    for piece in range(width // LANES):
        part = lax.dot_general(
            left_ref[:, piece * LANES : (piece + 1) * LANES], right_ref[...],
            (((0,), (0,)), ((), ())), preferred_element_type=F32,
        ).astype(out_ref.dtype)
        for i in range(LANES // share):
            for k in range(hid // LANES):
                start = ((piece * (LANES // share) + i) * hid // LANES + k) * share
                out_ref[start : start + share, :] = part[
                    i * share : (i + 1) * share, k * LANES : (k + 1) * LANES
                ]


def own_kernel(both_ref, side_ref, ends_ref, mine_ref, tail_ref):
    core, copy = core_place(), copy_place()
    keys = tail_ref.shape[0]
    width = ends_ref.shape[2]
    height = ends_ref.shape[1] // (2 * keys)
    weight_part(side_ref.at[core, copy], both_ref.at[core], mine_ref)
    for key in range(keys):
        start = 0
        rows = pl.ds(pl.multiple_of((copy * keys + key) * height, height), height)
        for t in range(2):
            for k in range(width // LANES):
                tail_ref[key, start : start + height, :] = ends_ref[
                    t, rows, k * LANES : (k + 1) * LANES
                ]
                start += height


def core_kernel(mine_ref, tail_ref, small_ref, other_ref, msg_ref):
    keys, tail = tail_ref.shape[:2]
    slab = mine_ref.shape[0] // keys
    small = join_small(split_small(small_ref[...])) + join_small(other_ref[keys * slab :, :])
    packed = split_small(small)
    for key in range(keys):
        here = slice(key * slab, (key + 1) * slab)
        msg_ref[key, :slab, :] = (mine_ref[here, :] + other_ref[here, :].astype(F32)).astype(BF16)
        msg_ref[key, slab : slab + tail, :] = tail_ref[key]
        msg_ref[key, slab + tail :, :] = packed


def slice_kernel(scaling, got_ref, slice_ref):
    share, hid = slice_ref.shape
    for k in range(hid // LANES):
        here = slice(k * share, (k + 1) * share)
        total = got_ref[0, here, :].astype(F32)
        for key in range(1, got_ref.shape[0]):
            total += got_ref[key, here, :].astype(F32)
        slice_ref[:, k * LANES : (k + 1) * LANES] = (total * scaling).astype(slice_ref.dtype)


def rows_kernel(
    start, scaling, got_ref, gate_ref, final_ref, grad_ref, pre_ref, gain_ref, mix_ref, gout_ref
):
    keys = got_ref.shape[0]
    own = final_ref.shape[0] // keys
    for out_ref in (final_ref, grad_ref):
        for k in range(final_ref.shape[1] // LANES):
            for key in range(keys):
                out_ref[key * own : (key + 1) * own, k * LANES : (k + 1) * LANES] = got_ref[
                    key, start : start + own, :
                ]
            start += own
    small = join_small(got_ref[0, start:, :])
    for key in range(1, keys):
        small = small + join_small(got_ref[key, start:, :])
    small = small * scaling
    gate = 1.0 / (1.0 + jnp.exp(-gate_ref[...]))
    first = 0
    for out_ref in (pre_ref, gain_ref, mix_ref, gout_ref):
        count = out_ref.shape[0]
        part = small[first : first + count]
        if out_ref is gout_ref:
            part = part * gate * (1.0 - gate)
        out_ref[...] = part
        first += count


def spread_kernel(flip, slice_ref, *refs):
    out_ref = refs[-1]
    copy = copy_place()
    for key in range(out_ref.shape[0]):
        out_ref[key, 1 - copy if flip else copy] = slice_ref[...]


def move_weight(source_ref, target_ref, sems):
    keys, copies = source_ref.shape[:2]
    moves = [
        pltpu.make_async_copy(
            source_ref.at[key, copy], target_ref.at[copy, key], sems.at[copies * key + copy]
        )
        for key in range(keys)
        for copy in range(copies)
    ]
    for move in moves:
        move.start()
    for move in moves:
        move.wait()


def mine_kernel(mine_ref, first_ref, second_ref, sems):
    for core, out_ref in enumerate((first_ref, second_ref)):

        @pl.when(core_place() == core)
        def _():
            move_weight(mine_ref, out_ref, sems)


def other_kernel(other_ref, first_in, second_in, first_ref, second_ref, sems):
    for core, out_ref in enumerate((second_ref, first_ref)):

        @pl.when(core_place() == core)
        def _():
            move_weight(other_ref, out_ref, sems)


def bit_groups(devices, bits):
    masks = [sum(1 << b for i, b in enumerate(bits) if j >> i & 1) for j in range(2 ** len(bits))]
    every = sum(1 << b for b in bits)
    return [[base | m for m in masks] for base in range(devices) if not base & every]


def exchange(value, devices, bits):
    groups = None if 2 ** len(bits) == devices else bit_groups(devices, bits)
    return lax.all_to_all(value, "seq", 0, 0, axis_index_groups=groups)


def send(value, devices, mask):
    return lax.ppermute(value, "seq", [(i, i ^ mask) for i in range(devices)])


VMEM = pl.BlockSpec(memory_space=pltpu.VMEM)
HBM = pl.BlockSpec(memory_space=pltpu.HBM)
PARAMS = pltpu.CompilerParams(vmem_limit_bytes=4 * 1024 * 1024)
WIDE = pltpu.CompilerParams(vmem_limit_bytes=32 * 1024 * 1024)


def compute(rows, kept):
    hid = kept[0].shape[1]
    count, own, double = rows.shape
    width = double // 2
    pairs = count * own // 2
    small_rows = (2 * hid + 4 * width) // LANES
    return pl.pallas_call(
        switch_kernel,
        out_shape=[
            jax.ShapeDtypeStruct((width * hid // LANES + 2 * small_rows, LANES), BF16),
            jax.ShapeDtypeStruct((2, LAYERS * pairs, hid), BF16),
            jax.ShapeDtypeStruct((2, 2, LAYERS * pairs, width), BF16),
            jax.ShapeDtypeStruct((2, 2 * pairs, width), BF16),
            jax.ShapeDtypeStruct((small_rows, LANES), F32),
        ],
        in_specs=[VMEM] * 7,
        out_specs=[VMEM] * 5,
        scratch_shapes=[
            pltpu.VMEM((pairs, hid), F32),
            pltpu.VMEM((LAYERS * pairs, hid), F32),
            pltpu.VMEM((LAYERS * pairs, hid), F32),
            pltpu.VMEM((LAYERS * pairs, LANES), F32),
            pltpu.VMEM((3, pairs, LANES), F32),
        ],
        compiler_params=WIDE,
        name="switch_layers",
    )(rows, *kept)


def per_device(tokens, cotangent, weight_in, bias_in, norm_gain, weight_out, bias_out, gate_logit):
    rows_dev, width = tokens.shape
    hid = weight_in.shape[1]
    devices = lax.axis_size("seq")
    top_bit = devices.bit_length() - 1
    top_bits = list(range(top_bit - LAYERS, top_bit))
    key_bits, copy_bit = top_bits[:-1], top_bits[-1]
    keys = 2 ** len(key_bits)
    own = rows_dev // keys

    kept = (weight_in, bias_in[None], norm_gain[None], weight_out, bias_out[None], gate_logit[None])
    kept = pl.pallas_call(
        keep_kernel,
        out_shape=[jax.ShapeDtypeStruct(k.shape, k.dtype) for k in kept],
        in_specs=[VMEM] * len(kept),
        out_specs=[VMEM] * len(kept),
        compiler_params=PARAMS,
        name="keep_weights",
    )(*kept)
    both = jnp.concatenate([tokens, cotangent], axis=-1).reshape(keys, own, 2 * width)
    rows = exchange(jnp.concatenate([both, both], axis=0), devices, top_bits)

    sent, both_sides, sides, ends, small = compute(rows, kept)
    received = send(sent, devices, 1)
    mine, tail = pl.pallas_call(
        own_kernel,
        out_shape=[
            jax.ShapeDtypeStruct((width * hid // LANES, LANES), F32),
            jax.ShapeDtypeStruct((keys, 2 * own * width // LANES, LANES), BF16),
        ],
        in_specs=[VMEM] * 3,
        out_specs=[VMEM] * 2,
        compiler_params=PARAMS,
        name="own_part",
    )(both_sides, sides, ends)
    message = pl.pallas_call(
        core_kernel,
        out_shape=jax.ShapeDtypeStruct(
            (keys, mine.shape[0] // keys + tail.shape[1] + 2 * small.shape[0], LANES), BF16
        ),
        in_specs=[VMEM] * 4,
        out_specs=VMEM,
        compiler_params=PARAMS,
        name="core_sum",
    )(mine, tail, small, received)
    share = width // keys
    got = exchange(message, devices, key_bits)
    scaling = float(rows_dev * devices // 2) ** (-0.5)
    rest = list(range(1, top_bit - LAYERS))
    rows_shape = jax.ShapeDtypeStruct((rows_dev, width), BF16)
    tall, short = hid // LANES, 2 * width // LANES
    owned = pl.pallas_call(
        functools.partial(slice_kernel, scaling),
        out_shape=jax.ShapeDtypeStruct((share, hid), F32 if rest else BF16),
        in_specs=[VMEM],
        out_specs=VMEM,
        compiler_params=PARAMS,
        name="slice_sum",
    )(got)
    final_rows, grad_rows, *small = pl.pallas_call(
        functools.partial(rows_kernel, share * hid // LANES, scaling),
        out_shape=[rows_shape] * 2
        + [jax.ShapeDtypeStruct((n, LANES), F32) for n in (tall, tall, short, short)],
        in_specs=[VMEM] * 2,
        out_specs=[VMEM] * 6,
        compiler_params=PARAMS,
        name="rows_out",
    )(got, kept[5].reshape(-1, LANES))
    if rest:
        owned, *small = lax.psum(
            (owned, *small), "seq", axis_index_groups=bit_groups(devices, rest)
        )
        owned = owned.astype(BF16)

    twin = send(owned, devices, 1 << copy_bit)
    spread_shape = jax.ShapeDtypeStruct((keys, 2, share, hid), BF16)
    spread = pl.pallas_call(
        functools.partial(spread_kernel, False),
        out_shape=spread_shape,
        in_specs=[VMEM],
        out_specs=VMEM,
        compiler_params=PARAMS,
        name="spread_own",
    )(owned)
    spread = pl.pallas_call(
        functools.partial(spread_kernel, True),
        out_shape=spread_shape,
        in_specs=[VMEM, VMEM],
        out_specs=VMEM,
        input_output_aliases={1: 0},
        compiler_params=PARAMS,
        name="spread_twin",
    )(twin, spread)
    whole = exchange(spread, devices, key_bits)
    other = send(whole, devices, 1)
    ordered = jax.ShapeDtypeStruct((2, keys, share, hid), BF16)
    weights = pl.pallas_call(
        mine_kernel,
        out_shape=[ordered] * 2,
        in_specs=[VMEM],
        out_specs=[HBM] * 2,
        scratch_shapes=[pltpu.SemaphoreType.DMA((2 * keys,))],
        compiler_params=PARAMS,
        name="mine_out",
    )(whole)
    grad_weight_in, grad_weight_out = pl.pallas_call(
        other_kernel,
        out_shape=[ordered] * 2,
        in_specs=[VMEM, HBM, HBM],
        out_specs=[HBM] * 2,
        scratch_shapes=[pltpu.SemaphoreType.DMA((2 * keys,))],
        input_output_aliases={1: 0, 2: 1},
        compiler_params=PARAMS,
        name="other_out",
    )(other, *weights)
    return (
        final_rows,
        grad_rows,
        grad_weight_in.reshape(2 * width, hid),
        grad_weight_out.reshape(2 * width, hid),
        *(s.reshape(-1) for s in small),
    )


def solution(mesh):
    placed = (P("seq", None), P("seq", None), P(), P(), P(), P(), P(), P())
    return jax.shard_map(
        per_device,
        mesh=mesh,
        in_specs=placed,
        out_specs=(P("seq", None), P("seq", None), P(), P(), P(), P(), P(), P()),
        check_vma=False,
    )
```

```python
import functools

import jax
import jax.numpy as jnp
from jax import lax
from jax.experimental import pallas as pl
from jax.experimental.pallas import tpu as pltpu
from jax.sharding import PartitionSpec as P

LAYERS = 4
LANES = 128
CHUNK = 16
TILE = 256

epsilon = 1e-05
branch_scale = 0.25
GELU_IN = 0.7978845608028654
GELU_CUBE = 0.044715

BF16 = jnp.bfloat16
F32 = jnp.float32


def split_small(total):
    high = total.astype(BF16).astype(F32)
    return jnp.concatenate([high, total - high], axis=0).astype(BF16)


def join_small(packed):
    wide = packed.astype(F32)
    rows = wide.shape[0] // 2
    return wide[:rows] + wide[rows:]


def layer_halves(blocks, layer):
    lower = [b for b in range(len(blocks)) if not b >> layer & 1]
    upper = [b for b in range(len(blocks)) if b >> layer & 1]
    left = jnp.concatenate([blocks[b] for b in lower], axis=0)
    right = jnp.concatenate([blocks[b] for b in upper], axis=0)
    return jnp.concatenate([left, right], axis=1), lower, upper


def layer_blocks(joined, lower, upper, height, width):
    blocks = [None] * (2 * len(lower))
    for i, b in enumerate(lower):
        blocks[b] = joined[i * height : (i + 1) * height, :width]
    for i, b in enumerate(upper):
        blocks[b] = joined[i * height : (i + 1) * height, width:]
    return blocks


def keep_kernel(*refs):
    half = len(refs) // 2
    for source, target in zip(refs[:half], refs[half:]):
        target[...] = source[...]


def fold_lanes(tile):
    return sum(tile[:, k : k + LANES] for k in range(0, tile.shape[1], LANES))


def widen(stat):
    return jnp.concatenate([stat] * (TILE // LANES), axis=1)


def row_total(folded):
    return jnp.sum(folded, axis=-1, keepdims=True)


def core_place():
    return lax.axis_index("seq") & 1


def copy_place():
    return lax.axis_index("seq") >> (lax.axis_size("seq").bit_length() - 2) & 1


def output_vectors(vectors_ref, width):
    begin = vectors_ref.shape[1] - 4 * width
    bias_out = vectors_ref[:, begin : begin + 2 * width]
    return bias_out, 1.0 / (1.0 + jnp.exp(-vectors_ref[:, begin + 2 * width :]))


def layer_result(paired, hidden_ref, wout_ref, gate, bias_out):
    mixed = lax.dot_general(
        hidden_ref[...], wout_ref[...], (((1,), (1,)), ((), ())), preferred_element_type=F32
    )
    return (gate * paired.astype(F32) + branch_scale * (mixed + bias_out)).astype(BF16)


def layer_grads(grad_out, cast_ref, win_ref, gate):
    back_in = lax.dot_general(
        cast_ref[...], win_ref[...], (((1,), (1,)), ((), ())), preferred_element_type=F32
    )
    return (gate * grad_out.astype(F32) + back_in).astype(BF16)


def switch_kernel(
    rows_ref, win_ref, wout_ref, vectors_ref,
    send_ref, both_s, side_s, first_ref, small_ref,
    pre_s, normed_s, slope_s, inv_s, stat_s,
):
    core, copy = core_place(), copy_place()
    count, height, double = rows_ref.shape
    width = double // 2
    pairs = count * height // 2
    hid = win_ref.shape[1]
    keys = count // 2
    columns = [slice(c, c + TILE) for c in range(0, hid, TILE)]
    chunks = [slice(r, r + CHUNK) for r in range(0, pairs, CHUNK)]
    bin_ref, gain_ref = vectors_ref.at[:, :hid], vectors_ref.at[:, hid : 2 * hid]
    bias_out, gate = output_vectors(vectors_ref, width)

    def below(layer, here):
        return slice(layer * pairs + here.start, layer * pairs + here.stop)

    blocks = [rows_ref[b, :, :width] for b in range(count)]
    for layer in range(LAYERS):
        paired, lower, upper = layer_halves(blocks, layer)
        span = slice(layer * pairs, (layer + 1) * pairs)
        for side in range(2):
            side_s[0, side, span, :] = paired[:, side * width : (side + 1) * width]

        def project(column):
            pre_s[:, column] = jnp.dot(
                paired, win_ref[:, column], preferred_element_type=F32
            ) + bin_ref[:, column]

        def gather_stats(column):
            for here in chunks:
                pre = pre_s[here, column]
                if column.start == 0:
                    shift = row_total(fold_lanes(pre)) * (1.0 / TILE)
                    stat_s[0, here, :] = jnp.broadcast_to(shift, (CHUNK, LANES))
                    moved = pre - shift
                    stat_s[1, here, :] = fold_lanes(moved)
                    stat_s[2, here, :] = fold_lanes(moved * moved)
                else:
                    moved = pre - widen(stat_s[0, here, :])
                    stat_s[1, here, :] += fold_lanes(moved)
                    stat_s[2, here, :] += fold_lanes(moved * moved)

        project(columns[0])
        for now, column in zip(columns[1:], columns):
            project(now)
            gather_stats(column)
        gather_stats(columns[-1])
        for here in chunks:
            drift = row_total(stat_s[1, here, :]) * (1.0 / hid)
            square = row_total(stat_s[2, here, :]) * (1.0 / hid)
            inv_std = lax.rsqrt(square - drift * drift + epsilon)
            stat_s[0, here, :] = stat_s[0, here, :] + drift
            inv_s[below(layer, here), :] = jnp.broadcast_to(inv_std, (CHUNK, LANES))
        def activate(column):
            for here in chunks:
                there = below(layer, here)
                normed = (pre_s[here, column] - widen(stat_s[0, here, :])) * widen(
                    inv_s[there, :]
                )
                scaled = normed * gain_ref[:, column]
                square = scaled * scaled
                bent = jnp.tanh(scaled * (GELU_IN + (GELU_IN * GELU_CUBE) * square))
                half = 0.5 + 0.5 * bent
                both_s[1, there, column] = (scaled * half).astype(BF16)
                slope_s[there, column] = half + (scaled * (0.5 - 0.5 * bent * bent)) * (
                    GELU_IN + (3.0 * GELU_IN * GELU_CUBE) * square
                )
                normed_s[there, column] = normed

        for column in columns:
            activate(column)
        if layer + 1 < LAYERS:
            result = layer_result(paired, both_s.at[1, span], wout_ref, gate, bias_out)
            blocks = layer_blocks(result, lower, upper, height, width)

    blocks = [rows_ref[b, :, width:] for b in range(count)]
    sum_pre = [jnp.zeros((1, TILE), F32) for _ in columns]
    sum_gain = [jnp.zeros((1, TILE), F32) for _ in columns]
    sum_mix = jnp.zeros((1, 2 * width), F32)
    sum_gate = jnp.zeros((1, 2 * width), F32)
    for layer in reversed(range(LAYERS)):
        grad_out, lower, upper = layer_halves(blocks, layer)
        span = slice(layer * pairs, (layer + 1) * pairs)
        out_grads = grad_out.astype(F32)
        paired = jnp.concatenate([side_s[0, side, span, :] for side in range(2)], axis=1)
        sum_gate += jnp.sum(out_grads * paired.astype(F32), axis=0, keepdims=True)
        mix_grads = branch_scale * out_grads
        sum_mix += jnp.sum(mix_grads, axis=0, keepdims=True)
        mix_cast = mix_grads.astype(BF16)
        for side in range(2):
            side_s[1, side, span, :] = mix_cast[:, side * width : (side + 1) * width]

        def project(column):
            pre_s[:, column] = jnp.dot(
                mix_cast, wout_ref[:, column], preferred_element_type=F32
            )

        def gather_stats(i, column):
            gains = jnp.zeros((CHUNK, TILE), F32)
            for here in chunks:
                there = below(layer, here)
                normed = normed_s[there, column]
                scaled_grads = slope_s[there, column] * pre_s[here, column]
                gains += scaled_grads * normed
                normed_grads = scaled_grads * gain_ref[:, column]
                pre_s[here, column] = normed_grads
                first = fold_lanes(normed_grads)
                second = fold_lanes(normed_grads * normed)
                if i == 0:
                    stat_s[1, here, :] = first
                    stat_s[2, here, :] = second
                else:
                    stat_s[1, here, :] += first
                    stat_s[2, here, :] += second
            sum_gain[i] += jnp.sum(gains, axis=0, keepdims=True)

        project(columns[0])
        for i, now in enumerate(columns[1:]):
            project(now)
            gather_stats(i, columns[i])
        gather_stats(len(columns) - 1, columns[-1])
        for here in chunks:
            for k in (1, 2):
                mean = row_total(stat_s[k, here, :]) * (1.0 / hid)
                stat_s[k, here, :] = jnp.broadcast_to(mean, (CHUNK, LANES))
        def finish(i, column):
            total = jnp.zeros((CHUNK, TILE), F32)
            for here in chunks:
                there = below(layer, here)
                pre_grads = widen(inv_s[there, :]) * (
                    pre_s[here, column]
                    - widen(stat_s[1, here, :])
                    - normed_s[there, column] * widen(stat_s[2, here, :])
                )
                total += pre_grads
                both_s[0, there, column] = pre_grads.astype(BF16)
            sum_pre[i] += jnp.sum(total, axis=0, keepdims=True)

        for i, column in enumerate(columns):
            finish(i, column)
        if layer:
            result = layer_grads(grad_out, both_s.at[0, span], win_ref, gate)
            blocks = layer_blocks(result, lower, upper, height, width)
    first_ref[...] = grad_out

    weight_part(side_s.at[1 - core, copy], both_s.at[1 - core], send_ref)
    row = 0
    for total in (*sum_pre, *sum_gain, sum_mix, sum_gate):
        for k in range(total.shape[1] // LANES):
            small_ref[row : row + 1, :] = total[:, k * LANES : (k + 1) * LANES]
            row += 1
    packed = split_small(small_ref[...])
    send_ref[send_ref.shape[0] - packed.shape[0] :, :] = packed


def weight_part(left_ref, right_ref, out_ref):
    width, hid = left_ref.shape[1], right_ref.shape[1]
    share = 2 * width // 2**LAYERS
    for piece in range(width // LANES):
        part = lax.dot_general(
            left_ref[:, piece * LANES : (piece + 1) * LANES], right_ref[...],
            (((0,), (0,)), ((), ())), preferred_element_type=F32,
        ).astype(out_ref.dtype)
        for i in range(LANES // share):
            for k in range(hid // LANES):
                start = ((piece * (LANES // share) + i) * hid // LANES + k) * share
                out_ref[start : start + share, :] = part[
                    i * share : (i + 1) * share, k * LANES : (k + 1) * LANES
                ]


def own_kernel(
    both_ref, side_ref, first_ref, win_ref, wout_ref, vectors_ref, mine_ref, tail_ref, ends_s
):
    core, copy = core_place(), copy_place()
    keys = tail_ref.shape[0]
    width = ends_s.shape[2]
    height = ends_s.shape[1] // (2 * keys)
    pairs = first_ref.shape[0]
    weight_part(side_ref.at[core, copy], both_ref.at[core], mine_ref)
    bias_out, gate = output_vectors(vectors_ref, width)
    last = slice((LAYERS - 1) * pairs, LAYERS * pairs)
    paired = jnp.concatenate([side_ref[0, side, last, :] for side in range(2)], axis=1)
    result = layer_result(paired, both_ref.at[1, last], wout_ref, gate, bias_out)
    grads = layer_grads(first_ref[...], both_ref.at[0, :pairs], win_ref, gate)
    for t, layer, joined in ((0, LAYERS - 1, result), (1, 0, grads)):
        lower = [b for b in range(2 * keys) if not b >> layer & 1]
        upper = [b for b in range(2 * keys) if b >> layer & 1]
        for b, block in enumerate(layer_blocks(joined, lower, upper, height, width)):
            ends_s[t, b * height : (b + 1) * height, :] = block
    for key in range(keys):
        start = 0
        rows = pl.ds(pl.multiple_of((copy * keys + key) * height, height), height)
        for t in range(2):
            for k in range(width // LANES):
                tail_ref[key, start : start + height, :] = ends_s[
                    t, rows, k * LANES : (k + 1) * LANES
                ]
                start += height


def core_kernel(mine_ref, tail_ref, small_ref, other_ref, msg_ref):
    keys, tail = tail_ref.shape[:2]
    slab = mine_ref.shape[0] // keys
    small = join_small(split_small(small_ref[...])) + join_small(other_ref[keys * slab :, :])
    packed = split_small(small)
    for key in range(keys):
        here = slice(key * slab, (key + 1) * slab)
        msg_ref[key, :slab, :] = (mine_ref[here, :] + other_ref[here, :].astype(F32)).astype(BF16)
        msg_ref[key, slab : slab + tail, :] = tail_ref[key]
        msg_ref[key, slab + tail :, :] = packed


def slice_kernel(scaling, got_ref, slice_ref):
    share, hid = slice_ref.shape
    for k in range(hid // LANES):
        here = slice(k * share, (k + 1) * share)
        total = got_ref[0, here, :].astype(F32)
        for key in range(1, got_ref.shape[0]):
            total += got_ref[key, here, :].astype(F32)
        slice_ref[:, k * LANES : (k + 1) * LANES] = (total * scaling).astype(slice_ref.dtype)


def rows_kernel(
    start, scaling, got_ref, vectors_ref, final_ref, grad_ref, pre_ref, gain_ref, mix_ref, gout_ref
):
    keys = got_ref.shape[0]
    own = final_ref.shape[0] // keys
    for out_ref in (final_ref, grad_ref):
        for k in range(final_ref.shape[1] // LANES):
            for key in range(keys):
                out_ref[key * own : (key + 1) * own, k * LANES : (k + 1) * LANES] = got_ref[
                    key, start : start + own, :
                ]
            start += own
    small = join_small(got_ref[0, start:, :])
    for key in range(1, keys):
        small = small + join_small(got_ref[key, start:, :])
    small = small * scaling
    count = gout_ref.shape[0]
    begin = vectors_ref.shape[1] - count * LANES
    logit = [vectors_ref[:, begin + k * LANES : begin + (k + 1) * LANES] for k in range(count)]
    gate = 1.0 / (1.0 + jnp.exp(-jnp.concatenate(logit, axis=0)))
    first = 0
    for out_ref in (pre_ref, gain_ref, mix_ref, gout_ref):
        count = out_ref.shape[0]
        part = small[first : first + count]
        if out_ref is gout_ref:
            part = part * gate * (1.0 - gate)
        out_ref[...] = part
        first += count


def spread_kernel(flip, slice_ref, *refs):
    out_ref = refs[-1]
    copy = copy_place()
    for key in range(out_ref.shape[0]):
        out_ref[key, 1 - copy if flip else copy] = slice_ref[...]


def move_weight(source_ref, target_ref, sems):
    keys, copies = source_ref.shape[:2]
    moves = [
        pltpu.make_async_copy(
            source_ref.at[key, copy], target_ref.at[copy, key], sems.at[copies * key + copy]
        )
        for key in range(keys)
        for copy in range(copies)
    ]
    for move in moves:
        move.start()
    for move in moves:
        move.wait()


def mine_kernel(mine_ref, first_ref, second_ref, sems):
    for core, out_ref in enumerate((first_ref, second_ref)):

        @pl.when(core_place() == core)
        def _():
            move_weight(mine_ref, out_ref, sems)


def other_kernel(other_ref, first_in, second_in, first_ref, second_ref, sems):
    for core, out_ref in enumerate((second_ref, first_ref)):

        @pl.when(core_place() == core)
        def _():
            move_weight(other_ref, out_ref, sems)


def bit_groups(devices, bits):
    masks = [sum(1 << b for i, b in enumerate(bits) if j >> i & 1) for j in range(2 ** len(bits))]
    every = sum(1 << b for b in bits)
    return [[base | m for m in masks] for base in range(devices) if not base & every]


def exchange(value, devices, bits):
    groups = None if 2 ** len(bits) == devices else bit_groups(devices, bits)
    return lax.all_to_all(value, "seq", 0, 0, axis_index_groups=groups)


def send(value, devices, mask):
    return lax.ppermute(value, "seq", [(i, i ^ mask) for i in range(devices)])


VMEM = pl.BlockSpec(memory_space=pltpu.VMEM)
HBM = pl.BlockSpec(memory_space=pltpu.HBM)
PARAMS = pltpu.CompilerParams(vmem_limit_bytes=4 * 1024 * 1024)
WIDE = pltpu.CompilerParams(vmem_limit_bytes=32 * 1024 * 1024)


def compute(rows, kept):
    hid = kept[0].shape[1]
    count, own, double = rows.shape
    width = double // 2
    pairs = count * own // 2
    small_rows = (2 * hid + 4 * width) // LANES
    return pl.pallas_call(
        switch_kernel,
        out_shape=[
            jax.ShapeDtypeStruct((width * hid // LANES + 2 * small_rows, LANES), BF16),
            jax.ShapeDtypeStruct((2, LAYERS * pairs, hid), BF16),
            jax.ShapeDtypeStruct((2, 2, LAYERS * pairs, width), BF16),
            jax.ShapeDtypeStruct((pairs, 2 * width), BF16),
            jax.ShapeDtypeStruct((small_rows, LANES), F32),
        ],
        in_specs=[VMEM] * 4,
        out_specs=[VMEM] * 5,
        scratch_shapes=[
            pltpu.VMEM((pairs, hid), F32),
            pltpu.VMEM((LAYERS * pairs, hid), F32),
            pltpu.VMEM((LAYERS * pairs, hid), F32),
            pltpu.VMEM((LAYERS * pairs, LANES), F32),
            pltpu.VMEM((3, pairs, LANES), F32),
        ],
        compiler_params=WIDE,
        name="switch_layers",
    )(rows, *kept)


def per_device(tokens, cotangent, weight_in, bias_in, norm_gain, weight_out, bias_out, gate_logit):
    rows_dev, width = tokens.shape
    hid = weight_in.shape[1]
    devices = lax.axis_size("seq")
    top_bit = devices.bit_length() - 1
    top_bits = list(range(top_bit - LAYERS, top_bit))
    key_bits, copy_bit = top_bits[:-1], top_bits[-1]
    keys = 2 ** len(key_bits)
    own = rows_dev // keys

    vectors = jnp.concatenate([bias_in, norm_gain, bias_out, gate_logit])[None]
    kept = (weight_in, weight_out, vectors)
    kept = pl.pallas_call(
        keep_kernel,
        out_shape=[jax.ShapeDtypeStruct(k.shape, k.dtype) for k in kept],
        in_specs=[VMEM] * len(kept),
        out_specs=[VMEM] * len(kept),
        compiler_params=PARAMS,
        name="keep_weights",
    )(*kept)
    both = jnp.concatenate([tokens, cotangent], axis=-1).reshape(keys, own, 2 * width)
    rows = exchange(jnp.concatenate([both, both], axis=0), devices, top_bits)

    sent, both_sides, sides, first, small = compute(rows, kept)
    received = send(sent, devices, 1)
    mine, tail = pl.pallas_call(
        own_kernel,
        out_shape=[
            jax.ShapeDtypeStruct((width * hid // LANES, LANES), F32),
            jax.ShapeDtypeStruct((keys, 2 * own * width // LANES, LANES), BF16),
        ],
        in_specs=[VMEM] * 6,
        out_specs=[VMEM] * 2,
        scratch_shapes=[pltpu.VMEM((2, 2 * keys * own, width), BF16)],
        compiler_params=WIDE,
        name="own_part",
    )(both_sides, sides, first, *kept)
    message = pl.pallas_call(
        core_kernel,
        out_shape=jax.ShapeDtypeStruct(
            (keys, mine.shape[0] // keys + tail.shape[1] + 2 * small.shape[0], LANES), BF16
        ),
        in_specs=[VMEM] * 4,
        out_specs=VMEM,
        compiler_params=PARAMS,
        name="core_sum",
    )(mine, tail, small, received)
    share = width // keys
    got = exchange(message, devices, key_bits)
    scaling = float(rows_dev * devices // 2) ** (-0.5)
    rest = list(range(1, top_bit - LAYERS))
    rows_shape = jax.ShapeDtypeStruct((rows_dev, width), BF16)
    tall, short = hid // LANES, 2 * width // LANES
    owned = pl.pallas_call(
        functools.partial(slice_kernel, scaling),
        out_shape=jax.ShapeDtypeStruct((share, hid), F32 if rest else BF16),
        in_specs=[VMEM],
        out_specs=VMEM,
        compiler_params=PARAMS,
        name="slice_sum",
    )(got)
    final_rows, grad_rows, *small = pl.pallas_call(
        functools.partial(rows_kernel, share * hid // LANES, scaling),
        out_shape=[rows_shape] * 2
        + [jax.ShapeDtypeStruct((n, LANES), F32) for n in (tall, tall, short, short)],
        in_specs=[VMEM] * 2,
        out_specs=[VMEM] * 6,
        compiler_params=PARAMS,
        name="rows_out",
    )(got, kept[2])
    if rest:
        owned, *small = lax.psum(
            (owned, *small), "seq", axis_index_groups=bit_groups(devices, rest)
        )
        owned = owned.astype(BF16)

    twin = send(owned, devices, 1 << copy_bit)
    spread_shape = jax.ShapeDtypeStruct((keys, 2, share, hid), BF16)
    spread = pl.pallas_call(
        functools.partial(spread_kernel, False),
        out_shape=spread_shape,
        in_specs=[VMEM],
        out_specs=VMEM,
        compiler_params=PARAMS,
        name="spread_own",
    )(owned)
    spread = pl.pallas_call(
        functools.partial(spread_kernel, True),
        out_shape=spread_shape,
        in_specs=[VMEM, VMEM],
        out_specs=VMEM,
        input_output_aliases={1: 0},
        compiler_params=PARAMS,
        name="spread_twin",
    )(twin, spread)
    whole = exchange(spread, devices, key_bits)
    other = send(whole, devices, 1)
    ordered = jax.ShapeDtypeStruct((2, keys, share, hid), BF16)
    weights = pl.pallas_call(
        mine_kernel,
        out_shape=[ordered] * 2,
        in_specs=[VMEM],
        out_specs=[HBM] * 2,
        scratch_shapes=[pltpu.SemaphoreType.DMA((2 * keys,))],
        compiler_params=PARAMS,
        name="mine_out",
    )(whole)
    grad_weight_in, grad_weight_out = pl.pallas_call(
        other_kernel,
        out_shape=[ordered] * 2,
        in_specs=[VMEM, HBM, HBM],
        out_specs=[HBM] * 2,
        scratch_shapes=[pltpu.SemaphoreType.DMA((2 * keys,))],
        input_output_aliases={1: 0, 2: 1},
        compiler_params=PARAMS,
        name="other_out",
    )(other, *weights)
    return (
        final_rows,
        grad_rows,
        grad_weight_in.reshape(2 * width, hid),
        grad_weight_out.reshape(2 * width, hid),
        *(s.reshape(-1) for s in small),
    )


def solution(mesh):
    placed = (P("seq", None), P("seq", None), P(), P(), P(), P(), P(), P())
    return jax.shard_map(
        per_device,
        mesh=mesh,
        in_specs=placed,
        out_specs=(P("seq", None), P("seq", None), P(), P(), P(), P(), P(), P()),
        check_vma=False,
    )
```

```python
import functools

import jax
import jax.numpy as jnp
from jax import lax
from jax.experimental import pallas as pl
from jax.experimental.pallas import tpu as pltpu
from jax.sharding import PartitionSpec as P

LAYERS = 4
LANES = 128
CHUNK = 16
TILE = 256

epsilon = 1e-05
branch_scale = 0.25
GELU_IN = 0.7978845608028654
GELU_CUBE = 0.044715

BF16 = jnp.bfloat16
F32 = jnp.float32


def slot_order(count):
    return [j // 2 if j % 2 == 0 else count - 1 - j // 2 for j in range(count)]


def split_small(total):
    high = total.astype(BF16).astype(F32)
    return jnp.concatenate([high, total - high], axis=0).astype(BF16)


def join_small(packed):
    wide = packed.astype(F32)
    rows = wide.shape[0] // 2
    return wide[:rows] + wide[rows:]


def layer_halves(blocks, layer):
    lower = [b for b in range(len(blocks)) if not b >> layer & 1]
    upper = [b for b in range(len(blocks)) if b >> layer & 1]
    left = jnp.concatenate([blocks[b] for b in lower], axis=0)
    right = jnp.concatenate([blocks[b] for b in upper], axis=0)
    return jnp.concatenate([left, right], axis=1), lower, upper


def layer_blocks(joined, lower, upper, height, width):
    blocks = [None] * (2 * len(lower))
    for i, b in enumerate(lower):
        blocks[b] = joined[i * height : (i + 1) * height, :width]
    for i, b in enumerate(upper):
        blocks[b] = joined[i * height : (i + 1) * height, width:]
    return blocks


def keep_kernel(*refs):
    half = len(refs) // 2
    for source, target in zip(refs[:half], refs[half:]):
        target[...] = source[...]


def fold_lanes(tile):
    return sum(tile[:, k : k + LANES] for k in range(0, tile.shape[1], LANES))


def widen(stat):
    return jnp.concatenate([stat] * (TILE // LANES), axis=1)


def row_total(folded):
    return jnp.sum(folded, axis=-1, keepdims=True)


def core_place():
    return lax.axis_index("seq") & 1


def copy_place():
    return lax.axis_index("seq") >> (lax.axis_size("seq").bit_length() - 2) & 1


def output_vectors(vectors_ref, width):
    begin = vectors_ref.shape[1] - 4 * width
    bias_out = vectors_ref[:, begin : begin + 2 * width]
    return bias_out, 1.0 / (1.0 + jnp.exp(-vectors_ref[:, begin + 2 * width :]))


def layer_result(paired, hidden_ref, wout_ref, gate, bias_out):
    mixed = lax.dot_general(
        hidden_ref[...], wout_ref[...], (((1,), (1,)), ((), ())), preferred_element_type=F32
    )
    return (gate * paired.astype(F32) + branch_scale * (mixed + bias_out)).astype(BF16)


def layer_grads(grad_out, cast_ref, win_ref, gate):
    back_in = lax.dot_general(
        cast_ref[...], win_ref[...], (((1,), (1,)), ((), ())), preferred_element_type=F32
    )
    return (gate * grad_out.astype(F32) + back_in).astype(BF16)


def switch_kernel(
    rows_ref, win_ref, wout_ref, vectors_ref,
    send_ref, both_s, side_s, first_ref, small_ref,
    pre_s, normed_s, slope_s, inv_s, stat_s,
):
    core, copy = core_place(), copy_place()
    count, height, double = rows_ref.shape
    width = double // 2
    pairs = count * height // 2
    hid = win_ref.shape[1]
    keys = count // 2
    columns = [slice(c, c + TILE) for c in range(0, hid, TILE)]
    chunks = [slice(r, r + CHUNK) for r in range(0, pairs, CHUNK)]
    bin_ref, gain_ref = vectors_ref.at[:, :hid], vectors_ref.at[:, hid : 2 * hid]
    bias_out, gate = output_vectors(vectors_ref, width)

    def below(layer, here):
        return slice(layer * pairs + here.start, layer * pairs + here.stop)

    blocks = [rows_ref[b, :, :width] for b in range(count)]
    for layer in range(LAYERS):
        paired, lower, upper = layer_halves(blocks, layer)
        span = slice(layer * pairs, (layer + 1) * pairs)
        for side in range(2):
            side_s[0, side, span, :] = paired[:, side * width : (side + 1) * width]

        def project(column):
            pre_s[:, column] = jnp.dot(
                paired, win_ref[:, column], preferred_element_type=F32
            ) + bin_ref[:, column]

        def gather_stats(column):
            for here in chunks:
                pre = pre_s[here, column]
                if column.start == 0:
                    shift = row_total(fold_lanes(pre)) * (1.0 / TILE)
                    stat_s[0, here, :] = jnp.broadcast_to(shift, (CHUNK, LANES))
                    moved = pre - shift
                    stat_s[1, here, :] = fold_lanes(moved)
                    stat_s[2, here, :] = fold_lanes(moved * moved)
                else:
                    moved = pre - widen(stat_s[0, here, :])
                    stat_s[1, here, :] += fold_lanes(moved)
                    stat_s[2, here, :] += fold_lanes(moved * moved)

        project(columns[0])
        for now, column in zip(columns[1:], columns):
            project(now)
            gather_stats(column)
        gather_stats(columns[-1])
        for here in chunks:
            drift = row_total(stat_s[1, here, :]) * (1.0 / hid)
            square = row_total(stat_s[2, here, :]) * (1.0 / hid)
            inv_std = lax.rsqrt(square - drift * drift + epsilon)
            stat_s[0, here, :] = stat_s[0, here, :] + drift
            inv_s[below(layer, here), :] = jnp.broadcast_to(inv_std, (CHUNK, LANES))
        def activate(column):
            for here in chunks:
                there = below(layer, here)
                normed = (pre_s[here, column] - widen(stat_s[0, here, :])) * widen(
                    inv_s[there, :]
                )
                scaled = normed * gain_ref[:, column]
                square = scaled * scaled
                bent = jnp.tanh(scaled * (GELU_IN + (GELU_IN * GELU_CUBE) * square))
                half = 0.5 + 0.5 * bent
                both_s[1, there, column] = (scaled * half).astype(BF16)
                slope_s[there, column] = half + (scaled * (0.5 - 0.5 * bent * bent)) * (
                    GELU_IN + (3.0 * GELU_IN * GELU_CUBE) * square
                )
                normed_s[there, column] = normed

        for column in columns:
            activate(column)
        if layer + 1 < LAYERS:
            result = layer_result(paired, both_s.at[1, span], wout_ref, gate, bias_out)
            blocks = layer_blocks(result, lower, upper, height, width)

    blocks = [rows_ref[b, :, width:] for b in range(count)]
    sum_pre = [jnp.zeros((1, TILE), F32) for _ in columns]
    sum_gain = [jnp.zeros((1, TILE), F32) for _ in columns]
    sum_mix = jnp.zeros((1, 2 * width), F32)
    sum_gate = jnp.zeros((1, 2 * width), F32)
    for layer in reversed(range(LAYERS)):
        grad_out, lower, upper = layer_halves(blocks, layer)
        span = slice(layer * pairs, (layer + 1) * pairs)
        out_grads = grad_out.astype(F32)
        paired = jnp.concatenate([side_s[0, side, span, :] for side in range(2)], axis=1)
        sum_gate += jnp.sum(out_grads * paired.astype(F32), axis=0, keepdims=True)
        mix_grads = branch_scale * out_grads
        sum_mix += jnp.sum(mix_grads, axis=0, keepdims=True)
        mix_cast = mix_grads.astype(BF16)
        for side in range(2):
            side_s[1, side, span, :] = mix_cast[:, side * width : (side + 1) * width]

        def project(column):
            pre_s[:, column] = jnp.dot(
                mix_cast, wout_ref[:, column], preferred_element_type=F32
            )

        def gather_stats(i, column):
            gains = jnp.zeros((CHUNK, TILE), F32)
            for here in chunks:
                there = below(layer, here)
                normed = normed_s[there, column]
                scaled_grads = slope_s[there, column] * pre_s[here, column]
                gains += scaled_grads * normed
                normed_grads = scaled_grads * gain_ref[:, column]
                pre_s[here, column] = normed_grads
                first = fold_lanes(normed_grads)
                second = fold_lanes(normed_grads * normed)
                if i == 0:
                    stat_s[1, here, :] = first
                    stat_s[2, here, :] = second
                else:
                    stat_s[1, here, :] += first
                    stat_s[2, here, :] += second
            sum_gain[i] += jnp.sum(gains, axis=0, keepdims=True)

        project(columns[0])
        for i, now in enumerate(columns[1:]):
            project(now)
            gather_stats(i, columns[i])
        gather_stats(len(columns) - 1, columns[-1])
        for here in chunks:
            for k in (1, 2):
                mean = row_total(stat_s[k, here, :]) * (1.0 / hid)
                stat_s[k, here, :] = jnp.broadcast_to(mean, (CHUNK, LANES))
        def finish(i, column):
            total = jnp.zeros((CHUNK, TILE), F32)
            for here in chunks:
                there = below(layer, here)
                pre_grads = widen(inv_s[there, :]) * (
                    pre_s[here, column]
                    - widen(stat_s[1, here, :])
                    - normed_s[there, column] * widen(stat_s[2, here, :])
                )
                total += pre_grads
                both_s[0, there, column] = pre_grads.astype(BF16)
            sum_pre[i] += jnp.sum(total, axis=0, keepdims=True)

        for i, column in enumerate(columns):
            finish(i, column)
        if layer:
            result = layer_grads(grad_out, both_s.at[0, span], win_ref, gate)
            blocks = layer_blocks(result, lower, upper, height, width)
    first_ref[...] = grad_out

    weight_part(side_s.at[1 - core, copy], both_s.at[1 - core], send_ref)
    row = 0
    for total in (*sum_pre, *sum_gain, sum_mix, sum_gate):
        for k in range(total.shape[1] // LANES):
            small_ref[row : row + 1, :] = total[:, k * LANES : (k + 1) * LANES]
            row += 1
    packed = split_small(small_ref[...])
    send_ref[send_ref.shape[0] - packed.shape[0] :, :] = packed


def weight_part(left_ref, right_ref, out_ref):
    width, hid = left_ref.shape[1], right_ref.shape[1]
    share = 2 * width // 2**LAYERS
    for piece in range(width // LANES):
        part = lax.dot_general(
            left_ref[:, piece * LANES : (piece + 1) * LANES], right_ref[...],
            (((0,), (0,)), ((), ())), preferred_element_type=F32,
        ).astype(out_ref.dtype)
        for i in range(LANES // share):
            for k in range(hid // LANES):
                start = ((piece * (LANES // share) + i) * hid // LANES + k) * share
                out_ref[start : start + share, :] = part[
                    i * share : (i + 1) * share, k * LANES : (k + 1) * LANES
                ]


def own_kernel(
    both_ref, side_ref, first_ref, win_ref, wout_ref, vectors_ref, mine_ref, tail_ref, ends_s
):
    core, copy = core_place(), copy_place()
    keys = tail_ref.shape[0]
    width = ends_s.shape[2]
    height = ends_s.shape[1] // (2 * keys)
    pairs = first_ref.shape[0]
    weight_part(side_ref.at[core, copy], both_ref.at[core], mine_ref)
    bias_out, gate = output_vectors(vectors_ref, width)
    last = slice((LAYERS - 1) * pairs, LAYERS * pairs)
    paired = jnp.concatenate([side_ref[0, side, last, :] for side in range(2)], axis=1)
    result = layer_result(paired, both_ref.at[1, last], wout_ref, gate, bias_out)
    grads = layer_grads(first_ref[...], both_ref.at[0, :pairs], win_ref, gate)
    for t, layer, joined in ((0, LAYERS - 1, result), (1, 0, grads)):
        lower = [b for b in range(2 * keys) if not b >> layer & 1]
        upper = [b for b in range(2 * keys) if b >> layer & 1]
        for b, block in enumerate(layer_blocks(joined, lower, upper, height, width)):
            ends_s[t, b * height : (b + 1) * height, :] = block
    for key in range(keys):
        start = 0
        rows = pl.ds(pl.multiple_of((copy * keys + key) * height, height), height)
        for t in range(2):
            for k in range(width // LANES):
                tail_ref[key, start : start + height, :] = ends_s[
                    t, rows, k * LANES : (k + 1) * LANES
                ]
                start += height


def core_kernel(mine_ref, tail_ref, small_ref, other_ref, msg_ref):
    keys, tail = tail_ref.shape[:2]
    slab = mine_ref.shape[0] // keys
    small = join_small(split_small(small_ref[...])) + join_small(other_ref[keys * slab :, :])
    packed = split_small(small)
    for slot, key in enumerate(slot_order(keys)):
        here = slice(key * slab, (key + 1) * slab)
        msg_ref[slot, :slab, :] = (mine_ref[here, :] + other_ref[here, :].astype(F32)).astype(BF16)
        msg_ref[slot, slab : slab + tail, :] = tail_ref[key]
        msg_ref[slot, slab + tail :, :] = packed


def slice_kernel(scaling, got_ref, slice_ref):
    share, hid = slice_ref.shape
    for k in range(hid // LANES):
        here = slice(k * share, (k + 1) * share)
        total = got_ref[0, here, :].astype(F32)
        for key in range(1, got_ref.shape[0]):
            total += got_ref[key, here, :].astype(F32)
        slice_ref[:, k * LANES : (k + 1) * LANES] = (total * scaling).astype(slice_ref.dtype)


def rows_kernel(
    start, scaling, got_ref, vectors_ref, final_ref, grad_ref, pre_ref, gain_ref, mix_ref, gout_ref
):
    keys = got_ref.shape[0]
    own = final_ref.shape[0] // keys
    for out_ref in (final_ref, grad_ref):
        for k in range(final_ref.shape[1] // LANES):
            for slot, key in enumerate(slot_order(keys)):
                out_ref[key * own : (key + 1) * own, k * LANES : (k + 1) * LANES] = got_ref[
                    slot, start : start + own, :
                ]
            start += own
    small = join_small(got_ref[0, start:, :])
    for key in range(1, keys):
        small = small + join_small(got_ref[key, start:, :])
    small = small * scaling
    count = gout_ref.shape[0]
    begin = vectors_ref.shape[1] - count * LANES
    logit = [vectors_ref[:, begin + k * LANES : begin + (k + 1) * LANES] for k in range(count)]
    gate = 1.0 / (1.0 + jnp.exp(-jnp.concatenate(logit, axis=0)))
    first = 0
    for out_ref in (pre_ref, gain_ref, mix_ref, gout_ref):
        count = out_ref.shape[0]
        part = small[first : first + count]
        if out_ref is gout_ref:
            part = part * gate * (1.0 - gate)
        out_ref[...] = part
        first += count


def spread_kernel(flip, slice_ref, *refs):
    out_ref = refs[-1]
    copy = copy_place()
    for key in range(out_ref.shape[0]):
        out_ref[key, 1 - copy if flip else copy] = slice_ref[...]


def move_weight(source_ref, target_ref, sems):
    keys, copies = source_ref.shape[:2]
    moves = [
        pltpu.make_async_copy(
            source_ref.at[slot, copy], target_ref.at[copy, key], sems.at[copies * key + copy]
        )
        for slot, key in enumerate(slot_order(keys))
        for copy in range(copies)
    ]
    for move in moves:
        move.start()
    for move in moves:
        move.wait()


def mine_kernel(mine_ref, first_ref, second_ref, sems):
    for core, out_ref in enumerate((first_ref, second_ref)):

        @pl.when(core_place() == core)
        def _():
            move_weight(mine_ref, out_ref, sems)


def other_kernel(other_ref, first_in, second_in, first_ref, second_ref, sems):
    for core, out_ref in enumerate((second_ref, first_ref)):

        @pl.when(core_place() == core)
        def _():
            move_weight(other_ref, out_ref, sems)


def bit_groups(devices, bits):
    masks = [sum(1 << b for i, b in enumerate(bits) if j >> i & 1) for j in range(2 ** len(bits))]
    every = sum(1 << b for b in bits)
    return [[base | m for m in masks] for base in range(devices) if not base & every]


def exchange(value, groups):
    return lax.all_to_all(value, "seq", 0, 0, axis_index_groups=groups)


def send(value, devices, mask):
    return lax.ppermute(value, "seq", [(i, i ^ mask) for i in range(devices)])


VMEM = pl.BlockSpec(memory_space=pltpu.VMEM)
HBM = pl.BlockSpec(memory_space=pltpu.HBM)
PARAMS = pltpu.CompilerParams(vmem_limit_bytes=4 * 1024 * 1024)
WIDE = pltpu.CompilerParams(vmem_limit_bytes=32 * 1024 * 1024)


def compute(rows, kept):
    hid = kept[0].shape[1]
    count, own, double = rows.shape
    width = double // 2
    pairs = count * own // 2
    small_rows = (2 * hid + 4 * width) // LANES
    return pl.pallas_call(
        switch_kernel,
        out_shape=[
            jax.ShapeDtypeStruct((width * hid // LANES + 2 * small_rows, LANES), BF16),
            jax.ShapeDtypeStruct((2, LAYERS * pairs, hid), BF16),
            jax.ShapeDtypeStruct((2, 2, LAYERS * pairs, width), BF16),
            jax.ShapeDtypeStruct((pairs, 2 * width), BF16),
            jax.ShapeDtypeStruct((small_rows, LANES), F32),
        ],
        in_specs=[VMEM] * 4,
        out_specs=[VMEM] * 5,
        scratch_shapes=[
            pltpu.VMEM((pairs, hid), F32),
            pltpu.VMEM((LAYERS * pairs, hid), F32),
            pltpu.VMEM((LAYERS * pairs, hid), F32),
            pltpu.VMEM((LAYERS * pairs, LANES), F32),
            pltpu.VMEM((3, pairs, LANES), F32),
        ],
        compiler_params=WIDE,
        name="switch_layers",
    )(rows, *kept)


def per_device(tokens, cotangent, weight_in, bias_in, norm_gain, weight_out, bias_out, gate_logit):
    rows_dev, width = tokens.shape
    hid = weight_in.shape[1]
    devices = lax.axis_size("seq")
    top_bit = devices.bit_length() - 1
    top_bits = list(range(top_bit - LAYERS, top_bit))
    key_bits, copy_bit = top_bits[:-1], top_bits[-1]
    keys = 2 ** len(key_bits)
    own = rows_dev // keys

    vectors = jnp.concatenate([bias_in, norm_gain, bias_out, gate_logit])[None]
    kept = (weight_in, weight_out, vectors)
    kept = pl.pallas_call(
        keep_kernel,
        out_shape=[jax.ShapeDtypeStruct(k.shape, k.dtype) for k in kept],
        in_specs=[VMEM] * len(kept),
        out_specs=[VMEM] * len(kept),
        compiler_params=PARAMS,
        name="keep_weights",
    )(*kept)
    both = jnp.concatenate([tokens, cotangent], axis=-1).reshape(keys, own, 2 * width)
    rows = exchange(jnp.concatenate([both, both], axis=0), bit_groups(devices, top_bits))

    sent, both_sides, sides, first, small = compute(rows, kept)
    received = send(sent, devices, 1)
    mine, tail = pl.pallas_call(
        own_kernel,
        out_shape=[
            jax.ShapeDtypeStruct((width * hid // LANES, LANES), F32),
            jax.ShapeDtypeStruct((keys, 2 * own * width // LANES, LANES), BF16),
        ],
        in_specs=[VMEM] * 6,
        out_specs=[VMEM] * 2,
        scratch_shapes=[pltpu.VMEM((2, 2 * keys * own, width), BF16)],
        compiler_params=WIDE,
        name="own_part",
    )(both_sides, sides, first, *kept)
    message = pl.pallas_call(
        core_kernel,
        out_shape=jax.ShapeDtypeStruct(
            (keys, mine.shape[0] // keys + tail.shape[1] + 2 * small.shape[0], LANES), BF16
        ),
        in_specs=[VMEM] * 4,
        out_specs=VMEM,
        compiler_params=PARAMS,
        name="core_sum",
    )(mine, tail, small, received)
    share = width // keys
    key_groups = [
        [group[key] for key in slot_order(keys)] for group in bit_groups(devices, key_bits)
    ]
    got = exchange(message, key_groups)
    scaling = float(rows_dev * devices // 2) ** (-0.5)
    rest = list(range(1, top_bit - LAYERS))
    rows_shape = jax.ShapeDtypeStruct((rows_dev, width), BF16)
    tall, short = hid // LANES, 2 * width // LANES
    owned = pl.pallas_call(
        functools.partial(slice_kernel, scaling),
        out_shape=jax.ShapeDtypeStruct((share, hid), F32 if rest else BF16),
        in_specs=[VMEM],
        out_specs=VMEM,
        compiler_params=PARAMS,
        name="slice_sum",
    )(got)
    final_rows, grad_rows, *small = pl.pallas_call(
        functools.partial(rows_kernel, share * hid // LANES, scaling),
        out_shape=[rows_shape] * 2
        + [jax.ShapeDtypeStruct((n, LANES), F32) for n in (tall, tall, short, short)],
        in_specs=[VMEM] * 2,
        out_specs=[VMEM] * 6,
        compiler_params=PARAMS,
        name="rows_out",
    )(got, kept[2])
    if rest:
        owned, *small = lax.psum(
            (owned, *small), "seq", axis_index_groups=bit_groups(devices, rest)
        )
        owned = owned.astype(BF16)

    twin = send(owned, devices, 1 << copy_bit)
    spread_shape = jax.ShapeDtypeStruct((keys, 2, share, hid), BF16)
    spread = pl.pallas_call(
        functools.partial(spread_kernel, False),
        out_shape=spread_shape,
        in_specs=[VMEM],
        out_specs=VMEM,
        compiler_params=PARAMS,
        name="spread_own",
    )(owned)
    spread = pl.pallas_call(
        functools.partial(spread_kernel, True),
        out_shape=spread_shape,
        in_specs=[VMEM, VMEM],
        out_specs=VMEM,
        input_output_aliases={1: 0},
        compiler_params=PARAMS,
        name="spread_twin",
    )(twin, spread)
    whole = exchange(spread, key_groups)
    other = send(whole, devices, 1)
    ordered = jax.ShapeDtypeStruct((2, keys, share, hid), BF16)
    weights = pl.pallas_call(
        mine_kernel,
        out_shape=[ordered] * 2,
        in_specs=[VMEM],
        out_specs=[HBM] * 2,
        scratch_shapes=[pltpu.SemaphoreType.DMA((2 * keys,))],
        compiler_params=PARAMS,
        name="mine_out",
    )(whole)
    grad_weight_in, grad_weight_out = pl.pallas_call(
        other_kernel,
        out_shape=[ordered] * 2,
        in_specs=[VMEM, HBM, HBM],
        out_specs=[HBM] * 2,
        scratch_shapes=[pltpu.SemaphoreType.DMA((2 * keys,))],
        input_output_aliases={1: 0, 2: 1},
        compiler_params=PARAMS,
        name="other_out",
    )(other, *weights)
    return (
        final_rows,
        grad_rows,
        grad_weight_in.reshape(2 * width, hid),
        grad_weight_out.reshape(2 * width, hid),
        *(s.reshape(-1) for s in small),
    )


def solution(mesh):
    placed = (P("seq", None), P("seq", None), P(), P(), P(), P(), P(), P())
    return jax.shard_map(
        per_device,
        mesh=mesh,
        in_specs=placed,
        out_specs=(P("seq", None), P("seq", None), P(), P(), P(), P(), P(), P()),
        check_vma=False,
    )
```

```python
import functools

import jax
import jax.numpy as jnp
from jax import lax
from jax.experimental import pallas as pl
from jax.experimental.pallas import tpu as pltpu
from jax.sharding import PartitionSpec as P

LAYERS = 4
LANES = 128
CHUNK = 16
TILE = 256

epsilon = 1e-05
branch_scale = 0.25
GELU_IN = 0.7978845608028654
GELU_CUBE = 0.044715

BF16 = jnp.bfloat16
F32 = jnp.float32


def slot_order(count):
    return [j // 2 if j % 2 == 0 else count - 1 - j // 2 for j in range(count)]


def split_small(total):
    high = total.astype(BF16).astype(F32)
    return jnp.concatenate([high, total - high], axis=0).astype(BF16)


def join_small(packed):
    wide = packed.astype(F32)
    rows = wide.shape[0] // 2
    return wide[:rows] + wide[rows:]


def layer_halves(blocks, layer):
    lower = [b for b in range(len(blocks)) if not b >> layer & 1]
    upper = [b for b in range(len(blocks)) if b >> layer & 1]
    left = jnp.concatenate([blocks[b] for b in lower], axis=0)
    right = jnp.concatenate([blocks[b] for b in upper], axis=0)
    return jnp.concatenate([left, right], axis=1), lower, upper


def layer_blocks(joined, lower, upper, height, width):
    blocks = [None] * (2 * len(lower))
    for i, b in enumerate(lower):
        blocks[b] = joined[i * height : (i + 1) * height, :width]
    for i, b in enumerate(upper):
        blocks[b] = joined[i * height : (i + 1) * height, width:]
    return blocks


def keep_kernel(*refs):
    half = len(refs) // 2
    for source, target in zip(refs[:half], refs[half:]):
        target[...] = source[...]


def fold_lanes(tile):
    return sum(tile[:, k : k + LANES] for k in range(0, tile.shape[1], LANES))


def widen(stat):
    return jnp.concatenate([stat] * (TILE // LANES), axis=1)


def row_total(folded):
    return jnp.sum(folded, axis=-1, keepdims=True)


def core_place():
    return lax.axis_index("seq") & 1


def copy_place():
    return lax.axis_index("seq") >> (lax.axis_size("seq").bit_length() - 2) & 1


def output_vectors(vectors_ref, width):
    begin = vectors_ref.shape[1] - 4 * width
    bias_out = vectors_ref[:, begin : begin + 2 * width]
    return bias_out, 1.0 / (1.0 + jnp.exp(-vectors_ref[:, begin + 2 * width :]))


def layer_result(paired, hidden_ref, wout_ref, gate, bias_out):
    mixed = lax.dot_general(
        hidden_ref[...], wout_ref[...], (((1,), (1,)), ((), ())), preferred_element_type=F32
    )
    return (gate * paired.astype(F32) + branch_scale * (mixed + bias_out)).astype(BF16)


def layer_grads(grad_out, cast_ref, win_ref, gate):
    back_in = lax.dot_general(
        cast_ref[...], win_ref[...], (((1,), (1,)), ((), ())), preferred_element_type=F32
    )
    return (gate * grad_out.astype(F32) + back_in).astype(BF16)


def switch_kernel(
    rows_ref, win_ref, wout_ref, vectors_ref,
    send_ref, both_s, side_s, first_ref, small_ref,
    pre_s, normed_s, slope_s, inv_s, stat_s,
):
    core, copy = core_place(), copy_place()
    count, height, double = rows_ref.shape
    width = double // 2
    pairs = count * height // 2
    hid = win_ref.shape[1]
    keys = count // 2
    columns = [slice(c, c + TILE) for c in range(0, hid, TILE)]
    chunks = [slice(r, r + CHUNK) for r in range(0, pairs, CHUNK)]
    bin_ref, gain_ref = vectors_ref.at[:, :hid], vectors_ref.at[:, hid : 2 * hid]
    bias_out, gate = output_vectors(vectors_ref, width)

    def below(layer, here):
        return slice(layer * pairs + here.start, layer * pairs + here.stop)

    blocks = [rows_ref[b, :, :width] for b in range(count)]
    for layer in range(LAYERS):
        paired, lower, upper = layer_halves(blocks, layer)
        span = slice(layer * pairs, (layer + 1) * pairs)
        for side in range(2):
            side_s[0, side, span, :] = paired[:, side * width : (side + 1) * width]

        def project(column):
            pre_s[:, column] = jnp.dot(
                paired, win_ref[:, column], preferred_element_type=F32
            ) + bin_ref[:, column]

        def gather_stats(column):
            for here in chunks:
                pre = pre_s[here, column]
                if column.start == 0:
                    shift = row_total(fold_lanes(pre)) * (1.0 / TILE)
                    stat_s[0, here, :] = jnp.broadcast_to(shift, (CHUNK, LANES))
                    moved = pre - shift
                    stat_s[1, here, :] = fold_lanes(moved)
                    stat_s[2, here, :] = fold_lanes(moved * moved)
                else:
                    moved = pre - widen(stat_s[0, here, :])
                    stat_s[1, here, :] += fold_lanes(moved)
                    stat_s[2, here, :] += fold_lanes(moved * moved)

        project(columns[0])
        for now, column in zip(columns[1:], columns):
            project(now)
            gather_stats(column)
        gather_stats(columns[-1])
        for here in chunks:
            drift = row_total(stat_s[1, here, :]) * (1.0 / hid)
            square = row_total(stat_s[2, here, :]) * (1.0 / hid)
            inv_std = lax.rsqrt(square - drift * drift + epsilon)
            stat_s[0, here, :] = stat_s[0, here, :] + drift
            inv_s[below(layer, here), :] = jnp.broadcast_to(inv_std, (CHUNK, LANES))
        def activate(column):
            for here in chunks:
                there = below(layer, here)
                normed = (pre_s[here, column] - widen(stat_s[0, here, :])) * widen(
                    inv_s[there, :]
                )
                scaled = normed * gain_ref[:, column]
                square = scaled * scaled
                bent = jnp.tanh(scaled * (GELU_IN + (GELU_IN * GELU_CUBE) * square))
                half = 0.5 + 0.5 * bent
                both_s[1, there, column] = (scaled * half).astype(BF16)
                slope_s[there, column] = half + (scaled * (0.5 - 0.5 * bent * bent)) * (
                    GELU_IN + (3.0 * GELU_IN * GELU_CUBE) * square
                )
                normed_s[there, column] = normed

        for column in columns:
            activate(column)
        if layer + 1 < LAYERS:
            result = layer_result(paired, both_s.at[1, span], wout_ref, gate, bias_out)
            blocks = layer_blocks(result, lower, upper, height, width)

    blocks = [rows_ref[b, :, width:] for b in range(count)]
    sum_pre = [jnp.zeros((1, TILE), F32) for _ in columns]
    sum_gain = [jnp.zeros((1, TILE), F32) for _ in columns]
    sum_mix = jnp.zeros((1, 2 * width), F32)
    sum_gate = jnp.zeros((1, 2 * width), F32)
    for layer in reversed(range(LAYERS)):
        grad_out, lower, upper = layer_halves(blocks, layer)
        span = slice(layer * pairs, (layer + 1) * pairs)
        out_grads = grad_out.astype(F32)
        paired = jnp.concatenate([side_s[0, side, span, :] for side in range(2)], axis=1)
        sum_gate += jnp.sum(out_grads * paired.astype(F32), axis=0, keepdims=True)
        mix_grads = branch_scale * out_grads
        sum_mix += jnp.sum(mix_grads, axis=0, keepdims=True)
        mix_cast = mix_grads.astype(BF16)
        for side in range(2):
            side_s[1, side, span, :] = mix_cast[:, side * width : (side + 1) * width]

        def project(column):
            pre_s[:, column] = jnp.dot(
                mix_cast, wout_ref[:, column], preferred_element_type=F32
            )

        def gather_stats(i, column):
            gains = jnp.zeros((CHUNK, TILE), F32)
            for here in chunks:
                there = below(layer, here)
                normed = normed_s[there, column]
                scaled_grads = slope_s[there, column] * pre_s[here, column]
                gains += scaled_grads * normed
                normed_grads = scaled_grads * gain_ref[:, column]
                pre_s[here, column] = normed_grads
                first = fold_lanes(normed_grads)
                second = fold_lanes(normed_grads * normed)
                if i == 0:
                    stat_s[1, here, :] = first
                    stat_s[2, here, :] = second
                else:
                    stat_s[1, here, :] += first
                    stat_s[2, here, :] += second
            sum_gain[i] += jnp.sum(gains, axis=0, keepdims=True)

        project(columns[0])
        for i, now in enumerate(columns[1:]):
            project(now)
            gather_stats(i, columns[i])
        gather_stats(len(columns) - 1, columns[-1])
        for here in chunks:
            for k in (1, 2):
                mean = row_total(stat_s[k, here, :]) * (1.0 / hid)
                stat_s[k, here, :] = jnp.broadcast_to(mean, (CHUNK, LANES))
        def finish(i, column):
            total = jnp.zeros((CHUNK, TILE), F32)
            for here in chunks:
                there = below(layer, here)
                pre_grads = widen(inv_s[there, :]) * (
                    pre_s[here, column]
                    - widen(stat_s[1, here, :])
                    - normed_s[there, column] * widen(stat_s[2, here, :])
                )
                total += pre_grads
                both_s[0, there, column] = pre_grads.astype(BF16)
            sum_pre[i] += jnp.sum(total, axis=0, keepdims=True)

        for i, column in enumerate(columns):
            finish(i, column)
        if layer:
            result = layer_grads(grad_out, both_s.at[0, span], win_ref, gate)
            blocks = layer_blocks(result, lower, upper, height, width)
    first_ref[...] = grad_out

    weight_part(side_s.at[1 - core, copy], both_s.at[1 - core], send_ref)
    row = 0
    for total in (*sum_pre, *sum_gain, sum_mix, sum_gate):
        for k in range(total.shape[1] // LANES):
            small_ref[row : row + 1, :] = total[:, k * LANES : (k + 1) * LANES]
            row += 1
    packed = split_small(small_ref[...])
    send_ref[send_ref.shape[0] - packed.shape[0] :, :] = packed


def weight_part(left_ref, right_ref, out_ref):
    width, hid = left_ref.shape[1], right_ref.shape[1]
    share = 2 * width // 2**LAYERS
    for piece in range(width // LANES):
        part = lax.dot_general(
            left_ref[:, piece * LANES : (piece + 1) * LANES], right_ref[...],
            (((0,), (0,)), ((), ())), preferred_element_type=F32,
        ).astype(out_ref.dtype)
        for i in range(LANES // share):
            for k in range(hid // LANES):
                start = ((piece * (LANES // share) + i) * hid // LANES + k) * share
                out_ref[start : start + share, :] = part[
                    i * share : (i + 1) * share, k * LANES : (k + 1) * LANES
                ]


def own_kernel(
    both_ref, side_ref, first_ref, win_ref, wout_ref, vectors_ref, mine_ref, tail_ref, ends_s
):
    core, copy = core_place(), copy_place()
    keys = tail_ref.shape[0]
    width = ends_s.shape[2]
    height = ends_s.shape[1] // (2 * keys)
    pairs = first_ref.shape[0]
    weight_part(side_ref.at[core, copy], both_ref.at[core], mine_ref)
    bias_out, gate = output_vectors(vectors_ref, width)
    last = slice((LAYERS - 1) * pairs, LAYERS * pairs)
    paired = jnp.concatenate([side_ref[0, side, last, :] for side in range(2)], axis=1)
    result = layer_result(paired, both_ref.at[1, last], wout_ref, gate, bias_out)
    grads = layer_grads(first_ref[...], both_ref.at[0, :pairs], win_ref, gate)
    for t, layer, joined in ((0, LAYERS - 1, result), (1, 0, grads)):
        lower = [b for b in range(2 * keys) if not b >> layer & 1]
        upper = [b for b in range(2 * keys) if b >> layer & 1]
        for b, block in enumerate(layer_blocks(joined, lower, upper, height, width)):
            ends_s[t, b * height : (b + 1) * height, :] = block
    for key in range(keys):
        start = 0
        rows = pl.ds(pl.multiple_of((copy * keys + key) * height, height), height)
        for t in range(2):
            for k in range(width // LANES):
                tail_ref[key, start : start + height, :] = ends_s[
                    t, rows, k * LANES : (k + 1) * LANES
                ]
                start += height


def core_kernel(mine_ref, tail_ref, small_ref, other_ref, msg_ref):
    keys, tail = tail_ref.shape[:2]
    slab = mine_ref.shape[0] // keys
    small = join_small(split_small(small_ref[...])) + join_small(other_ref[keys * slab :, :])
    packed = split_small(small)
    for slot, key in enumerate(slot_order(keys)):
        here = slice(key * slab, (key + 1) * slab)
        msg_ref[slot, :slab, :] = (mine_ref[here, :] + other_ref[here, :].astype(F32)).astype(BF16)
        msg_ref[slot, slab : slab + tail, :] = tail_ref[key]
        msg_ref[slot, slab + tail :, :] = packed


def slice_kernel(scaling, got_ref, slice_ref):
    share, hid = slice_ref.shape
    for k in range(hid // LANES):
        here = slice(k * share, (k + 1) * share)
        total = got_ref[0, here, :].astype(F32)
        for key in range(1, got_ref.shape[0]):
            total += got_ref[key, here, :].astype(F32)
        slice_ref[:, k * LANES : (k + 1) * LANES] = (total * scaling).astype(slice_ref.dtype)


def rows_kernel(
    start, scaling, got_ref, vectors_ref, final_ref, grad_ref, pre_ref, gain_ref, mix_ref, gout_ref
):
    keys = got_ref.shape[0]
    own = final_ref.shape[0] // keys
    for out_ref in (final_ref, grad_ref):
        for k in range(final_ref.shape[1] // LANES):
            for slot, key in enumerate(slot_order(keys)):
                out_ref[key * own : (key + 1) * own, k * LANES : (k + 1) * LANES] = got_ref[
                    slot, start : start + own, :
                ]
            start += own
    small = join_small(got_ref[0, start:, :])
    for key in range(1, keys):
        small = small + join_small(got_ref[key, start:, :])
    small = small * scaling
    count = gout_ref.shape[0]
    begin = vectors_ref.shape[1] - count * LANES
    logit = [vectors_ref[:, begin + k * LANES : begin + (k + 1) * LANES] for k in range(count)]
    gate = 1.0 / (1.0 + jnp.exp(-jnp.concatenate(logit, axis=0)))
    first = 0
    for out_ref in (pre_ref, gain_ref, mix_ref, gout_ref):
        count = out_ref.shape[0]
        part = small[first : first + count]
        if out_ref is gout_ref:
            part = part * gate * (1.0 - gate)
        out_ref[...] = part
        first += count


def spread_kernel(flip, slice_ref, *refs):
    out_ref = refs[-1]
    copy = copy_place()
    for key in range(out_ref.shape[0]):
        out_ref[key, 1 - copy if flip else copy] = slice_ref[...]


def move_weight(source_ref, target_ref, sems):
    keys, copies = source_ref.shape[:2]
    moves = [
        pltpu.make_async_copy(
            source_ref.at[key, copy], target_ref.at[copy, key], sems.at[copies * key + copy]
        )
        for key in range(keys)
        for copy in range(copies)
    ]
    for move in moves:
        move.start()
    for move in moves:
        move.wait()


def mine_kernel(mine_ref, first_ref, second_ref, sems):
    for core, out_ref in enumerate((first_ref, second_ref)):

        @pl.when(core_place() == core)
        def _():
            move_weight(mine_ref, out_ref, sems)


def other_kernel(other_ref, first_in, second_in, first_ref, second_ref, sems):
    for core, out_ref in enumerate((second_ref, first_ref)):

        @pl.when(core_place() == core)
        def _():
            move_weight(other_ref, out_ref, sems)


def bit_groups(devices, bits):
    masks = [sum(1 << b for i, b in enumerate(bits) if j >> i & 1) for j in range(2 ** len(bits))]
    every = sum(1 << b for b in bits)
    return [[base | m for m in masks] for base in range(devices) if not base & every]


def exchange(value, groups):
    return lax.all_to_all(value, "seq", 0, 0, axis_index_groups=groups)


def send(value, devices, mask):
    return lax.ppermute(value, "seq", [(i, i ^ mask) for i in range(devices)])


VMEM = pl.BlockSpec(memory_space=pltpu.VMEM)
HBM = pl.BlockSpec(memory_space=pltpu.HBM)
PARAMS = pltpu.CompilerParams(vmem_limit_bytes=4 * 1024 * 1024)
WIDE = pltpu.CompilerParams(vmem_limit_bytes=32 * 1024 * 1024)


def compute(rows, kept):
    hid = kept[0].shape[1]
    count, own, double = rows.shape
    width = double // 2
    pairs = count * own // 2
    small_rows = (2 * hid + 4 * width) // LANES
    return pl.pallas_call(
        switch_kernel,
        out_shape=[
            jax.ShapeDtypeStruct((width * hid // LANES + 2 * small_rows, LANES), BF16),
            jax.ShapeDtypeStruct((2, LAYERS * pairs, hid), BF16),
            jax.ShapeDtypeStruct((2, 2, LAYERS * pairs, width), BF16),
            jax.ShapeDtypeStruct((pairs, 2 * width), BF16),
            jax.ShapeDtypeStruct((small_rows, LANES), F32),
        ],
        in_specs=[VMEM] * 4,
        out_specs=[VMEM] * 5,
        scratch_shapes=[
            pltpu.VMEM((pairs, hid), F32),
            pltpu.VMEM((LAYERS * pairs, hid), F32),
            pltpu.VMEM((LAYERS * pairs, hid), F32),
            pltpu.VMEM((LAYERS * pairs, LANES), F32),
            pltpu.VMEM((3, pairs, LANES), F32),
        ],
        compiler_params=WIDE,
        name="switch_layers",
    )(rows, *kept)


def per_device(tokens, cotangent, weight_in, bias_in, norm_gain, weight_out, bias_out, gate_logit):
    rows_dev, width = tokens.shape
    hid = weight_in.shape[1]
    devices = lax.axis_size("seq")
    top_bit = devices.bit_length() - 1
    top_bits = list(range(top_bit - LAYERS, top_bit))
    key_bits, copy_bit = top_bits[:-1], top_bits[-1]
    keys = 2 ** len(key_bits)
    own = rows_dev // keys

    vectors = jnp.concatenate([bias_in, norm_gain, bias_out, gate_logit])[None]
    kept = (weight_in, weight_out, vectors)
    kept = pl.pallas_call(
        keep_kernel,
        out_shape=[jax.ShapeDtypeStruct(k.shape, k.dtype) for k in kept],
        in_specs=[VMEM] * len(kept),
        out_specs=[VMEM] * len(kept),
        compiler_params=PARAMS,
        name="keep_weights",
    )(*kept)
    both = jnp.concatenate([tokens, cotangent], axis=-1).reshape(keys, own, 2 * width)
    rows = exchange(jnp.concatenate([both, both], axis=0), bit_groups(devices, top_bits))

    sent, both_sides, sides, first, small = compute(rows, kept)
    received = send(sent, devices, 1)
    mine, tail = pl.pallas_call(
        own_kernel,
        out_shape=[
            jax.ShapeDtypeStruct((width * hid // LANES, LANES), F32),
            jax.ShapeDtypeStruct((keys, 2 * own * width // LANES, LANES), BF16),
        ],
        in_specs=[VMEM] * 6,
        out_specs=[VMEM] * 2,
        scratch_shapes=[pltpu.VMEM((2, 2 * keys * own, width), BF16)],
        compiler_params=WIDE,
        name="own_part",
    )(both_sides, sides, first, *kept)
    message = pl.pallas_call(
        core_kernel,
        out_shape=jax.ShapeDtypeStruct(
            (keys, mine.shape[0] // keys + tail.shape[1] + 2 * small.shape[0], LANES), BF16
        ),
        in_specs=[VMEM] * 4,
        out_specs=VMEM,
        compiler_params=PARAMS,
        name="core_sum",
    )(mine, tail, small, received)
    share = width // keys
    key_groups = [
        [group[key] for key in slot_order(keys)] for group in bit_groups(devices, key_bits)
    ]
    got = exchange(message, key_groups)
    scaling = float(rows_dev * devices // 2) ** (-0.5)
    rest = list(range(1, top_bit - LAYERS))
    rows_shape = jax.ShapeDtypeStruct((rows_dev, width), BF16)
    tall, short = hid // LANES, 2 * width // LANES
    owned = pl.pallas_call(
        functools.partial(slice_kernel, scaling),
        out_shape=jax.ShapeDtypeStruct((share, hid), F32 if rest else BF16),
        in_specs=[VMEM],
        out_specs=VMEM,
        compiler_params=PARAMS,
        name="slice_sum",
    )(got)
    final_rows, grad_rows, *small = pl.pallas_call(
        functools.partial(rows_kernel, share * hid // LANES, scaling),
        out_shape=[rows_shape] * 2
        + [jax.ShapeDtypeStruct((n, LANES), F32) for n in (tall, tall, short, short)],
        in_specs=[VMEM] * 2,
        out_specs=[VMEM] * 6,
        compiler_params=PARAMS,
        name="rows_out",
    )(got, kept[2])
    if rest:
        owned, *small = lax.psum(
            (owned, *small), "seq", axis_index_groups=bit_groups(devices, rest)
        )
        owned = owned.astype(BF16)

    twin = send(owned, devices, 1 << copy_bit)
    spread_shape = jax.ShapeDtypeStruct((keys, 2, share, hid), BF16)
    spread = pl.pallas_call(
        functools.partial(spread_kernel, False),
        out_shape=spread_shape,
        in_specs=[VMEM],
        out_specs=VMEM,
        compiler_params=PARAMS,
        name="spread_own",
    )(owned)
    spread = pl.pallas_call(
        functools.partial(spread_kernel, True),
        out_shape=spread_shape,
        in_specs=[VMEM, VMEM],
        out_specs=VMEM,
        input_output_aliases={1: 0},
        compiler_params=PARAMS,
        name="spread_twin",
    )(twin, spread)
    whole = exchange(spread, bit_groups(devices, key_bits))
    other = send(whole, devices, 1)
    ordered = jax.ShapeDtypeStruct((2, keys, share, hid), BF16)
    weights = pl.pallas_call(
        mine_kernel,
        out_shape=[ordered] * 2,
        in_specs=[VMEM],
        out_specs=[HBM] * 2,
        scratch_shapes=[pltpu.SemaphoreType.DMA((2 * keys,))],
        compiler_params=PARAMS,
        name="mine_out",
    )(whole)
    grad_weight_in, grad_weight_out = pl.pallas_call(
        other_kernel,
        out_shape=[ordered] * 2,
        in_specs=[VMEM, HBM, HBM],
        out_specs=[HBM] * 2,
        scratch_shapes=[pltpu.SemaphoreType.DMA((2 * keys,))],
        input_output_aliases={1: 0, 2: 1},
        compiler_params=PARAMS,
        name="other_out",
    )(other, *weights)
    return (
        final_rows,
        grad_rows,
        grad_weight_in.reshape(2 * width, hid),
        grad_weight_out.reshape(2 * width, hid),
        *(s.reshape(-1) for s in small),
    )


def solution(mesh):
    placed = (P("seq", None), P("seq", None), P(), P(), P(), P(), P(), P())
    return jax.shard_map(
        per_device,
        mesh=mesh,
        in_specs=placed,
        out_specs=(P("seq", None), P("seq", None), P(), P(), P(), P(), P(), P()),
        check_vma=False,
    )
```
